32 devices in a mesh: grp: 2 (over x), path: 16 (over z, y, core).
Axes of the slice: x: 2, y: 2, z: 4, core: 2. Of those that a mesh axis runs over, the one named last changes fastest.
Arguments:
- normals: float32 [32, 524288], P(None, ('grp', 'path')), may hold values from -10.1 to 10.1
- spot_today: float32 [32], replicated, may hold values from 0.5 to 2
- volatility: float32 [32], replicated, may hold values from 0.1 to 0.5
- weights: float32 [32], replicated, may hold values from 0.5 to 1.5
- cash_flows: float32 [524288], P(('grp', 'path')), may hold values from -300 to 300
- exercise: int32 [524288], P(('grp', 'path')), may hold values 0 or 1
Outputs:
- path_value: float32 [524288], P(('grp', 'path'))
- state_cot: float32 [32, 524288], P(None, ('grp', 'path'))
- flow_cot: float32 [524288], P(('grp', 'path'))
- greeks: float32 [2, 32], replicated
The draws below stay inside these ranges and needn't reach their ends.
All inputs are finite; a program needn't handle non-finite values. No bound on the sum of `exercise` on one device may be relied on, other than what follows from the above.
Results may differ from the reference program's by a relative error of at most 0.0003.
Values sent between devices are 32-bit elements; how exact they have to be, the bound alone decides.
No kernel may reach another device: no remote copies, remote signals or barrier semaphores. Data moves between devices by JAX's collectives and lax.ppermute only.
A program may use at most 64 MiB of HBM per device.

```python
import math
import jax
import jax.numpy as jnp
from jax import lax

ASSETS = 32
PATHS = 524288


def driving(key):
    base_key = jax.random.fold_in(key, 101)
    rough_key = jax.random.fold_in(key, 102)
    common_key = jax.random.fold_in(key, 104)
    base = jax.random.truncated_normal(base_key, -4.0, 4.0, (ASSETS, PATHS), jnp.float32)
    common = jax.random.truncated_normal(common_key, -4.0, 4.0, (PATHS,), jnp.float32)
    mixed = jnp.clip(0.6 * common[None, :] + 0.8 * base, -4.0, 4.0)
    position = jnp.arange(PATHS, dtype=jnp.float32) / PATHS
    rise = 0.6 * jnp.exp(math.log(3.0) * position)
    rough = jnp.exp(jax.random.uniform(rough_key, (PATHS,), jnp.float32, math.log(0.7), math.log(1.4)))
    return mixed * (rise * rough)[None, :]


def draw_normals(key, part):
    return driving(key)


def draw_cash_flows(key, part):
    moves = driving(key)
    noise = 0.5 * jax.random.truncated_normal(jax.random.fold_in(key, 103), -4.0, 4.0, (PATHS,), jnp.float32)
    neighbour = moves * jnp.roll(moves, -1, axis=0)
    signal = jnp.sum(0.5 * moves + 0.3 / math.sqrt(2.0) * (moves * moves - 1.0) + 0.2 * neighbour, axis=0) / math.sqrt(ASSETS)
    return signal + noise


def set_ends(array, rng, smallest, largest):
    longest = array.shape.index(max(array.shape))
    spots = []
    for shift in (0, 1):
        where = [jax.random.randint(jax.random.fold_in(rng, axis), (), 0, length) for axis, length in enumerate(array.shape)]
        where[longest] = (where[longest] + shift) % array.shape[longest]
        spots.append(tuple(where))
    return array.at[spots[0]].set(smallest).at[spots[1]].set(largest)


def setup_inputs(seed: int = 0) -> dict:
    key_of = jax.random.split(jax.random.key(seed), 7)
    return {
        "normals": draw_normals(jax.random.fold_in(key_of[6], 71), 0),
        "spot_today": jnp.clip(jnp.exp(jax.random.uniform(key_of[1], (ASSETS,), jnp.float32, math.log(0.5), math.log(2.0))), 0.5, 2.0),
        "volatility": jnp.clip(jnp.exp(jax.random.uniform(key_of[2], (ASSETS,), jnp.float32, math.log(0.1), math.log(0.5))), 0.1, 0.5),
        "weights": jnp.clip(jax.random.uniform(key_of[3], (ASSETS,), jnp.float32, 0.5, 1.5), 0.5, 1.5),
        "cash_flows": draw_cash_flows(jax.random.fold_in(key_of[6], 71), 0),
        "exercise": set_ends((jax.random.randint(key_of[5], (PATHS,), 0, 20) < 1).astype(jnp.int32), jax.random.fold_in(key_of[5], 1), 0, 1),
    }


expiry_time = 0.5
root_time = math.sqrt(0.5)
inv_root_two = 1.0 / math.sqrt(2.0)
notional = 20.0
soft_width = 0.02

def path_state(normals, spot_today, volatility):
    return spot_today[:, None] * jnp.exp(volatility[:, None] * (root_time * normals) - 0.5 * expiry_time * volatility[:, None] ** 2)

def basis_rows(state, spot_today, volatility):
    scaled = (state / spot_today[:, None] - 1.0) / (volatility[:, None] * root_time)
    leading = jnp.ones_like(scaled[:1])
    squares = (scaled * scaled - 1.0) * inv_root_two
    neighbour = scaled * jnp.roll(scaled, -1, axis=0)
    bounded = jnp.tanh(scaled[:-1])
    return jnp.concatenate([leading, scaled, squares, neighbour, bounded], axis=0)

def payoff(state, spot_today, weights):
    basket = lax.optimization_barrier(jnp.sum(weights[:, None] * state, axis=0)) / jnp.sum(weights * spot_today)
    return notional * soft_width * jax.nn.softplus((basket - 1.0) / soft_width)

def chol_solve(factor, rhs):
    first = lax.linalg.triangular_solve(factor, rhs, left_side=True, lower=True)
    return lax.linalg.triangular_solve(factor, first, left_side=True, lower=True, transpose_a=True)

def reference(normals, spot_today, volatility, weights, cash_flows, exercise):
    assets, paths = normals.shape
    features = 4 * assets
    block_width = math.gcd(paths, 65536)
    block_count = paths // block_width
    highest = lax.Precision.HIGHEST
    contract_last = (((1,), (1,)), ((), ()))

    def block_inputs(block_index):
        block_start = block_index * block_width
        draw_block = lax.dynamic_slice_in_dim(normals, block_start, block_width, 1)
        flow_block = lax.dynamic_slice_in_dim(cash_flows, block_start, block_width, 0)
        taken_flag = lax.dynamic_slice_in_dim(exercise, block_start, block_width, 0).astype(jnp.float32)
        return (draw_block, flow_block, taken_flag)

    def gram_step(running, block_index):
        gram_acc, moment_acc = running
        draw_block, flow_block, taken_flag = block_inputs(block_index)
        basis_block = basis_rows(path_state(draw_block, spot_today, volatility), spot_today, volatility)
        gram_acc = gram_acc + lax.dot_general(basis_block.astype(jnp.float32), basis_block.astype(jnp.float32), contract_last, precision=highest, preferred_element_type=jnp.float32)
        targets = jnp.stack([flow_block, 1.0 - taken_flag])
        moment_acc = moment_acc + lax.dot_general(targets.astype(jnp.float32), basis_block.astype(jnp.float32), contract_last, precision=highest, preferred_element_type=jnp.float32)
        return ((gram_acc, moment_acc), None)
    start_sums = (jnp.zeros((features, features), jnp.float32), jnp.zeros((2, features), jnp.float32))
    (gram_acc, moment_acc), _ = lax.scan(gram_step, start_sums, jnp.arange(block_count, dtype=jnp.int32))
    gram_mean = gram_acc / paths
    moment_mean = moment_acc / paths
    factor = jnp.linalg.cholesky(gram_mean)
    coefficients = chol_solve(factor, moment_mean.T)
    regression = coefficients[:, 0]
    multiplier = coefficients[:, 1]
    coef_rows = coefficients.T

    def adjoint_block(block_index):
        draw_block, flow_block, taken_flag = block_inputs(block_index)
        state, path_back = jax.vjp(lambda spot_level, spread: path_state(draw_block, spot_level, spread), spot_today, volatility)
        (basis_block, reward), feature_back = jax.vjp(lambda current, spot_level, spread: (basis_rows(current, spot_level, spread), payoff(current, spot_level, weights)), state, spot_today, volatility)
        fitted = lax.dot_general(coef_rows.astype(jnp.float32), basis_block.astype(jnp.float32), (((1,), (0,)), ((), ())), precision=highest, preferred_element_type=jnp.float32)
        continuation = fitted[0]
        lam_phi = fitted[1]
        value_block = taken_flag * reward + (1.0 - taken_flag) * continuation
        rows_bar = multiplier[:, None] * (flow_block - continuation)[None, :] + regression[:, None] * (1.0 - taken_flag - lam_phi)[None, :]
        state_bar, spot_bar, spread_bar = feature_back((rows_bar, taken_flag))
        spot_path, spread_path = path_back(state_bar)
        greek_part = jnp.stack([spot_bar + spot_path, spread_bar + spread_path])
        return (value_block, state_bar, lam_phi, greek_part)
    value_blocks, state_blocks, flow_blocks, greek_parts = lax.map(adjoint_block, jnp.arange(block_count, dtype=jnp.int32))
    path_value = value_blocks.reshape(paths)
    state_cot = jnp.transpose(state_blocks, (1, 0, 2)).reshape(assets, paths)
    flow_cot = flow_blocks.reshape(paths)
    greeks = lax.optimization_barrier(jnp.sum(greek_parts, axis=0)) / paths
    return (path_value, state_cot, flow_cot, greeks)
```

```python
import functools
import math

import jax
import jax.numpy as jnp
from jax import lax
from jax.experimental import pallas as pl
from jax.experimental.pallas import tpu as pltpu
from jax.sharding import PartitionSpec as P

root_time = math.sqrt(0.5)
notional = 20.0
soft_width = 0.02
LANES = 128
F32 = jnp.float32
BF16 = jnp.bfloat16
CONTRACT_LAST = (((1,), (1,)), ((), ()))


def column(row, count):
    rows = lax.broadcasted_iota(jnp.int32, (count, count), 0)
    cols = lax.broadcasted_iota(jnp.int32, (count, count), 1)
    wide = jnp.broadcast_to(row, (count, count))
    picked = jnp.sum(jnp.where(rows == cols, wide, 0.0), axis=1, keepdims=True)
    return jnp.broadcast_to(picked, (count, LANES))


def split(x):
    hi = x.astype(BF16)
    lo = (x - hi.astype(F32)).astype(BF16)
    return hi, lo


def sums_kernel(
    assets, width,
    normals, spot, vol, weights, cash, taken,
    scaled_out, bounded_out, value_out, slope_out, gram_out, jac_out,
    coef, rows, jac_hi, jac_lo, gram_acc, jac_acc, jac_low,
):
    step = pl.program_id(0)
    features = 4 * assets

    @pl.when(step == 0)
    def _():
        spread = column(vol[...] * root_time, assets)
        wide = column(weights[...] * spot[...], assets)
        total = jnp.sum(weights[...] * spot[...], axis=1, keepdims=True)
        coef[0] = spread
        coef[1] = 0.5 * spread * spread
        coef[2] = 1.0 / spread
        coef[3] = wide / jnp.broadcast_to(total, (assets, LANES))
        gram_acc[...] = jnp.zeros_like(gram_acc)
        jac_acc[...] = jnp.zeros_like(jac_acc)
        jac_low[...] = jnp.zeros_like(jac_low)

    last = lax.broadcasted_iota(jnp.int32, (assets, LANES), 0) == assets - 1
    slot = lax.broadcasted_iota(jnp.int32, (16, LANES), 0)
    for c in range(width // LANES):
        at = pl.ds(c * LANES, LANES)
        draw = normals[:, at]
        spread = coef[0]
        growth = jnp.exp(spread * draw - coef[1])
        scaled = (growth - 1.0) * coef[2]
        bounded = jnp.where(last, 1.0, jnp.tanh(scaled))
        scaled_out[:, at] = scaled
        bounded_out[:, at] = bounded
        after = pltpu.roll(scaled, assets - 1, 0)
        before = pltpu.roll(scaled, 1, 0)
        basis = jnp.concatenate([scaled, scaled * scaled - 1.0, scaled * after, bounded], axis=0)
        hi, lo = split(basis)
        rows[16 : 16 + features, at] = hi
        rows[16 + features : 16 + 2 * features, at] = lo
        slope = growth * (draw - spread) - scaled
        jac = jnp.concatenate(
            [slope, slope * scaled, slope * after, slope * (1.0 - bounded * bounded), slope * before],
            axis=0,
        )
        hi, lo = split(jac)
        jac_hi[:, at] = hi
        jac_lo[:, at] = lo
        basket = jnp.sum(growth * coef[3], axis=0, keepdims=True)
        x = (basket - 1.0) * (1.0 / soft_width)
        decay = jnp.exp(-jnp.abs(x))
        reward = (notional * soft_width) * (jnp.maximum(x, 0.0) + jnp.log1p(decay))
        inverse = 1.0 / (1.0 + decay)
        sigmoid = jnp.where(x >= 0.0, inverse, decay * inverse)
        flag = taken[:, at].astype(F32)
        flow = cash[:, at]
        pull = notional * flag * sigmoid
        value_out[:, at] = flag * reward
        slope_out[:, at] = pull
        flow_hi = flow.astype(BF16).astype(F32)
        pull_hi = pull.astype(BF16).astype(F32)
        target = jnp.zeros((16, LANES), F32)
        for index, row in enumerate([flow_hi, flow - flow_hi, 1.0 - flag, pull_hi, pull - pull_hi]):
            target = jnp.where(slot == index, jnp.broadcast_to(row, (16, LANES)), target)
        rows[0:16, at] = target.astype(BF16)

    upper = rows[0 : 16 + features, :]
    gram_acc[...] += lax.dot_general(
        upper, rows[16:, :], CONTRACT_LAST, preferred_element_type=F32
    )
    jac_acc[...] += lax.dot_general(rows[...], jac_hi[...], CONTRACT_LAST, preferred_element_type=F32)
    jac_low[...] += lax.dot_general(upper, jac_lo[...], CONTRACT_LAST, preferred_element_type=F32)

    def targets(t):
        pairs = [t[0:1] + t[1:2], t[2:3], t[3:4] + t[4:5], jnp.zeros((5, t.shape[1]), F32)]
        return jnp.concatenate(pairs, axis=0)

    @pl.when(step == pl.num_programs(0) - 1)
    def _():
        high = gram_acc[16:, 0:features]
        half = 0.5 * high + gram_acc[16:, features:]
        gram_out[0:features, :] = half + half.T
        gram_out[features:, :] = targets(gram_acc[0:16, 0:features] + gram_acc[0:16, features:])
        both = jac_acc[16 : 16 + features, :] + jac_acc[16 + features :, :] + jac_low[16:, :]
        aims = targets(jac_acc[0:16, :] + jac_low[0:16, :])
        jac_out[0:features, :] = both[:, 0:features]
        jac_out[features : features + assets, :] = jnp.concatenate(
            [both[assets * g : assets * (g + 1), features:] for g in range(4)], axis=1
        )
        jac_out[features + assets : features + assets + 8, :] = aims[:, 0:features]
        jac_out[features + assets + 8 :, :] = jnp.concatenate(
            [aims[:, features:], jnp.zeros((8, features - assets), F32)], axis=1
        )


def lane(block, index):
    return jnp.broadcast_to(block[:, index : index + 1], block.shape)


def solve_kernel(scale, gram, out, spread):
    features = gram.shape[1]
    blocks = features // 8
    lanes = lax.broadcasted_iota(jnp.int32, (8, features), 1)
    subs = lax.broadcasted_iota(jnp.int32, (8, features), 0)
    mat = [gram[8 * v : 8 * v + 8, :] * scale for v in range(blocks + 1)]
    for k in range(blocks):
        base = 8 * k
        head = mat[k]
        diag = {}
        for j in range(8):
            col = lane(head, base + j)
            spread[0, j] = col
            for i in range(j + 1):
                diag[i, j] = jnp.broadcast_to(spread[0, j, i : i + 1, :], (8, features))
        inside = (lanes >= base) & (lanes < base + 8)
        spread[1, 0] = jnp.where(inside, jnp.where(lanes == base + subs, -1.0, 0.0), head)
        work = [jnp.broadcast_to(spread[1, 0, i : i + 1, :], (8, features)) for i in range(8)]
        inverse, low = [], {}
        for p in range(8):
            inv = 1.0 / diag[p, p]
            inverse.append(inv)
            for j in range(p + 1, 8):
                low[p, j] = diag[p, j] * inv
            for i in range(p + 1, 8):
                for j in range(i, 8):
                    diag[i, j] = diag[i, j] - low[p, i] * diag[p, j]
                work[i] = work[i] - low[p, i] * work[p]
        for i in reversed(range(8)):
            value = work[i] * inverse[i]
            for j in range(i + 1, 8):
                value = value - low[i, j] * work[j]
            work[i] = value
        for v in range(k + 1, blocks + 1):
            new = jnp.where(inside, 0.0, mat[v])
            for c in range(8):
                new = new - lane(mat[v], base + c) * work[c]
            mat[v] = new
    kept = jnp.broadcast_to(gram[features + 2 : features + 3, :], (8, features))
    out[...] = jnp.where(subs == 3, kept, mat[blocks])


def adjoint_kernel(
    assets, width, path_total,
    scaled_in, bounded_in, cash, taken, value_in, pull_in, solved, jac, spot, vol, weights,
    value_out, cot_out, flow_out, greeks_out,
    coef,
):
    step = pl.program_id(0)
    features = 4 * assets

    @pl.when(step == 0)
    def _():
        turned = solved[...].T
        spread = column(vol[...] * root_time, assets)
        base = column(spot[...], assets)
        weight = column(weights[...], assets)
        total = jnp.sum(weights[...] * spot[...], axis=1, keepdims=True)
        gain = 1.0 / (base * spread)
        for which in range(2):
            parts = [
                jnp.broadcast_to(turned[assets * g : assets * (g + 1), which : which + 1], (assets, LANES))
                for g in range(4)
            ]
            at = 9 * which
            for g in range(4):
                coef[at + g] = parts[g]
            coef[at + 4] = parts[0] * gain
            coef[at + 5] = 2.0 * parts[1] * gain
            coef[at + 6] = parts[2] * gain
            coef[at + 7] = pltpu.roll(parts[2], 1, 0) * gain
            coef[at + 8] = parts[3] * gain
            offset = jnp.sum(parts[1], axis=0, keepdims=True)
            coef[19, 8 * which : 8 * which + 8] = jnp.broadcast_to(offset, (8, LANES))
        coef[18] = weight / jnp.broadcast_to(total, (assets, LANES))

    for c in range(width // LANES):
        at = pl.ds(c * LANES, LANES)
        scaled = scaled_in[:, at]
        bounded = bounded_in[:, at]
        after = pltpu.roll(scaled, assets - 1, 0)
        before = pltpu.roll(scaled, 1, 0)
        curve = 1.0 - bounded * bounded
        fitted, tangent = [], []
        for which in range(2):
            k = 9 * which
            inner = coef[k] + coef[k + 1] * scaled + coef[k + 2] * after
            terms = scaled * inner + coef[k + 3] * bounded
            fitted.append(jnp.sum(terms, axis=0, keepdims=True) - coef[19, 8 * which : 8 * which + 1])
            tangent.append(
                coef[k + 4] + coef[k + 5] * scaled + coef[k + 6] * after + coef[k + 7] * before
                + coef[k + 8] * curve
            )
        continuation, lam = fitted
        rest = 1.0 - taken[:, at].astype(F32)
        value_out[:, at] = value_in[:, at] + rest * continuation
        flow_out[:, at] = lam
        miss = cash[:, at] - continuation
        gap = rest - lam
        cot_out[:, at] = miss * tangent[1] + gap * tangent[0] + pull_in[:, at] * coef[18]

    @pl.when(step == pl.num_programs(0) - 1)
    def _():
        turned = solved[...].T
        regression, multiplier = solved[0:1, :], solved[1:2, :]
        group = lax.broadcasted_iota(jnp.int32, (assets, LANES), 1) // assets

        def against(which):
            main = jnp.sum(jac[0:features, :] * turned[:, which : which + 1], axis=0, keepdims=True)
            packed = jnp.zeros((assets, LANES), F32)
            for g in range(4):
                part = turned[assets * g : assets * (g + 1), which : which + 1]
                packed = jnp.where(group == g, jnp.broadcast_to(part, (assets, LANES)), packed)
            side = jnp.sum(jac[features : features + assets, :] * packed, axis=0, keepdims=True)
            side = side + pltpu.roll(side, 2 * assets, 1)
            side = side + pltpu.roll(side, assets, 1)
            return main, side

        aims = features + assets
        main_r, side_r = against(0)
        main_m, side_m = against(1)
        miss, gap = jac[aims : aims + 1, :] - main_r, jac[aims + 1 : aims + 2, :] - main_m
        miss_side = jac[aims + 8 : aims + 9, :] - side_r
        gap_side = jac[aims + 9 : aims + 10, :] - side_m
        lanes = lax.broadcasted_iota(jnp.int32, (1, LANES), 1)
        double = jnp.where((lanes >= assets) & (lanes < 2 * assets), 2.0, 1.0)
        total = double * (multiplier * miss + regression * gap)
        total = total + pltpu.roll(total, 2 * assets, 1)
        total = total + pltpu.roll(total, assets, 1)

        def earlier(row):
            moved = pltpu.roll(row, features - 2 * assets + 1, 1)
            wrapped = pltpu.roll(row, features - 3 * assets + 1, 1)
            return jnp.where(lanes == 0, wrapped, moved)

        total = total + earlier(multiplier) * miss_side + earlier(regression) * gap_side
        vega = total[:, 0:assets] / vol[...]
        pulled_slope = jac[aims + 2 : aims + 3, 0:assets]
        pulled_scaled = solved[3:4, 0:assets]
        pulled = solved[3:4, features - 1 : features]
        value = weights[...] * spot[...]
        whole = jnp.sum(value, axis=1, keepdims=True)
        growth = pulled + vol[...] * root_time * pulled_scaled
        mean = jnp.sum(value * growth, axis=1, keepdims=True) / whole
        delta = weights[...] / whole * (growth - mean)
        vega = vega + value * root_time / whole * (pulled_slope + pulled_scaled)
        greeks_out[...] = jnp.concatenate([delta, vega], axis=0) * (1.0 / path_total)


def add_up(values, axes):
    for axis in axes:
        size = lax.axis_size(axis)
        if size & (size - 1):
            values = [lax.psum(v, axis) for v in values]
            continue
        bit = 1
        while bit < size:
            pairs = [(i, i ^ bit) for i in range(size)]
            values = [v + lax.ppermute(v, axis, pairs) for v in values]
            bit *= 2
    return values


def per_device(normals, spot, vol, weights, cash, taken):
    assets, paths = normals.shape
    features = 4 * assets
    path_total = paths * lax.axis_size("grp") * lax.axis_size("path")
    width = math.gcd(paths, 2048)
    grid = (paths // width,)
    spot, vol, weights = (a.reshape(1, assets) for a in (spot, vol, weights))
    cash, taken = cash.reshape(1, paths), taken.reshape(1, paths)
    whole = pl.BlockSpec((1, assets), lambda i: (0, 0))
    line = pl.BlockSpec((1, width), lambda i: (0, i))
    tile = pl.BlockSpec((assets, width), lambda i: (0, i))
    full = lambda *shape: pl.BlockSpec(shape, lambda i: (0, 0))
    params = pltpu.CompilerParams(vmem_limit_bytes=48 * 1024 * 1024)
    big = jax.ShapeDtypeStruct((assets, paths), F32)
    row = jax.ShapeDtypeStruct((1, paths), F32)
    jac_rows = features + assets + 16
    scaled, bounded, value, pull, gram, jac = pl.pallas_call(
        functools.partial(sums_kernel, assets, width),
        grid=grid,
        in_specs=[tile, whole, whole, whole, line, line],
        out_specs=[tile, tile, line, line, full(features + 8, features), full(jac_rows, features)],
        out_shape=[
            big, big, row, row,
            jax.ShapeDtypeStruct((features + 8, features), F32),
            jax.ShapeDtypeStruct((jac_rows, features), F32),
        ],
        scratch_shapes=[
            pltpu.VMEM((4, assets, LANES), F32),
            pltpu.VMEM((16 + 2 * features, width), BF16),
            pltpu.VMEM((5 * assets, width), BF16),
            pltpu.VMEM((5 * assets, width), BF16),
            pltpu.VMEM((16 + features, 2 * features), F32),
            pltpu.VMEM((16 + 2 * features, 5 * assets), F32),
            pltpu.VMEM((16 + features, 5 * assets), F32),
        ],
        compiler_params=params,
        name="sums",
    )(normals, spot, vol, weights, cash, taken)
    gram, jac = add_up([gram, jac], ("path", "grp"))
    solved = pl.pallas_call(
        functools.partial(solve_kernel, 1.0 / path_total),
        out_shape=jax.ShapeDtypeStruct((8, features), F32),
        scratch_shapes=[pltpu.VMEM((2, 8, 8, features), F32)],
        compiler_params=params,
        name="solve",
    )(gram)
    value, cot, flow, greeks = pl.pallas_call(
        functools.partial(adjoint_kernel, assets, width, path_total),
        grid=grid,
        in_specs=[
            tile, tile, line, line, line, line,
            full(8, features), full(jac_rows, features), whole, whole, whole,
        ],
        out_specs=[line, tile, line, full(2, assets)],
        out_shape=[row, big, row, jax.ShapeDtypeStruct((2, assets), F32)],
        scratch_shapes=[pltpu.VMEM((20, assets, LANES), F32)],
        compiler_params=params,
        name="adjoint",
    )(scaled, bounded, cash, taken, value, pull, solved, jac, spot, vol, weights)
    return value.reshape(paths), cot, flow.reshape(paths), greeks


def solution(mesh):
    in_specs = (P(None, ("grp", "path")), P(), P(), P(), P(("grp", "path")), P(("grp", "path")))
    out_specs = (P(("grp", "path")), P(None, ("grp", "path")), P(("grp", "path")), P())
    return jax.shard_map(
        per_device, mesh=mesh, in_specs=in_specs, out_specs=out_specs, check_vma=False
    )
```

```python
import functools
import math

import jax
import jax.numpy as jnp
from jax import lax
from jax.experimental import pallas as pl
from jax.experimental.pallas import tpu as pltpu
from jax.sharding import PartitionSpec as P

root_time = math.sqrt(0.5)
notional = 20.0
soft_width = 0.02
LANES = 128
F32 = jnp.float32
BF16 = jnp.bfloat16
AXES = ("grp", "path")
CONTRACT_LAST = (((1,), (1,)), ((), ()))


def column(row, count):
    rows = lax.broadcasted_iota(jnp.int32, (count, count), 0)
    cols = lax.broadcasted_iota(jnp.int32, (count, count), 1)
    wide = jnp.broadcast_to(row, (count, count))
    picked = jnp.sum(jnp.where(rows == cols, wide, 0.0), axis=1, keepdims=True)
    return jnp.broadcast_to(picked, (count, LANES))


def split(x):
    hi = x.astype(BF16)
    lo = (x - hi.astype(F32)).astype(BF16)
    return hi, lo


def halves(rows):
    odd = lax.axis_index("path") & 1
    at = lambda index: pl.ds(pl.multiple_of(index * rows, 8), rows)
    return at(odd), at(1 - odd)


def sums_kernel(
    assets, width, spot, vol, weights, cash, taken, normals,
    scaled_out, bounded_out, value_out, pull_out, gram_out, jac_keep, jac_give,
    small, flows, flags, draws, coef, part, target,
    scaled_all, bounded_all, rows_a, tilts_a, rows_b, tilts_b, gram_acc, jac_acc, jac_low, jac, sems, sent,
):
    features = 4 * assets
    paths = draws.shape[1]
    chunks = width // LANES
    blocks = paths // width
    copies = [
        pltpu.make_async_copy(spot, small.at[0:1, :], sems.at[0]),
        pltpu.make_async_copy(vol, small.at[1:2, :], sems.at[1]),
        pltpu.make_async_copy(weights, small.at[2:3, :], sems.at[2]),
        pltpu.make_async_copy(cash, flows, sems.at[3]),
        pltpu.make_async_copy(taken, flags, sems.at[4]),
    ]

    def pair(index):
        at = pl.ds(pl.multiple_of(index * (2 * width), 2 * width), 2 * width)
        return pltpu.make_async_copy(normals.at[:, at], draws.at[:, at], sems.at[5 + index])

    def leave(index):
        at = pl.ds(pl.multiple_of(index * (2 * width), 2 * width), 2 * width)
        return [
            pltpu.make_async_copy(scaled_all.at[:, at], scaled_out.at[:, at], sent.at[0, index]),
            pltpu.make_async_copy(bounded_all.at[:, at], bounded_out.at[:, at], sent.at[1, index]),
        ]

    for copy in copies[:3]:
        copy.start()
    for index in range(blocks // 2):
        pair(index).start()
        if index == 0:
            for copy in copies[3:]:
                copy.start()
    gram_acc[...] = jnp.zeros_like(gram_acc)
    jac_acc[...] = jnp.zeros_like(jac_acc)
    jac_low[...] = jnp.zeros_like(jac_low)
    rows_b[...] = jnp.zeros_like(rows_b)
    tilts_b[...] = jnp.zeros_like(tilts_b)
    target[...] = jnp.zeros_like(target)
    for copy in copies[:3]:
        copy.wait()
    spread = column(small[1:2, :] * root_time, assets)
    value = small[2:3, :] * small[0:1, :]
    total = jnp.sum(value, axis=1, keepdims=True)
    coef[0] = spread
    coef[1] = 0.5 * spread * spread
    coef[2] = 1.0 / spread
    coef[3] = column(value, assets) / jnp.broadcast_to(total, (assets, LANES))
    for copy in copies[3:]:
        copy.wait()

    last = lax.broadcasted_iota(jnp.int32, (assets, LANES), 0) == assets - 1

    def fill(block, rows, tilts):
        for c in range(chunks):
            at = pl.ds(pl.multiple_of(block * width, width) + c * LANES, LANES)
            here = pl.ds(c * LANES, LANES)
            draw = draws[:, at]
            spread = coef[0]
            growth = jnp.exp(spread * draw - coef[1])
            weighted = growth * coef[3]
            part[8 * c : 8 * c + 8, :] = sum(weighted[8 * g : 8 * g + 8] for g in range(assets // 8))
            scaled = (growth - 1.0) * coef[2]
            bounded = jnp.where(last, 1.0, jnp.tanh(scaled))
            scaled_all[:, at] = scaled
            bounded_all[:, at] = bounded
            after = pltpu.roll(scaled, assets - 1, 0)
            before = pltpu.roll(scaled, 1, 0)
            basis = jnp.concatenate(
                [scaled, scaled * scaled - 1.0, scaled * after, bounded], axis=0
            )
            hi, lo = split(basis)
            rows[16 : 16 + features, here] = hi
            rows[16 + features : 16 + 2 * features, here] = lo
            slope = growth * (draw - spread) - scaled
            curve = 1.0 - bounded * bounded
            hi, lo = split(
                jnp.concatenate(
                    [slope, slope * scaled, slope * after, slope * curve, slope * before], axis=0
                )
            )
            tilts[0 : 5 * assets, here] = hi
            tilts[5 * assets : 10 * assets, here] = lo
        line = pl.ds(pl.multiple_of(block * chunks, chunks), chunks)
        basket = sum(part[pl.ds(i, chunks, stride=8), :] for i in range(8))
        x = (basket - 1.0) * (1.0 / soft_width)
        decay = jnp.exp(-jnp.abs(x))
        reward = (notional * soft_width) * (jnp.maximum(x, 0.0) + jnp.log1p(decay))
        inverse = 1.0 / (1.0 + decay)
        sigmoid = jnp.where(x >= 0.0, inverse, decay * inverse)
        flag = flags[line, :].astype(F32)
        flow = flows[line, :]
        pull = notional * flag * sigmoid
        value_out[line, :] = flag * reward
        pull_out[line, :] = pull
        flow_hi = flow.astype(BF16).astype(F32)
        pull_hi = pull.astype(BF16).astype(F32)
        for c in range(chunks):
            here = pl.ds(c * LANES, LANES)
            for index, row in enumerate(
                [flow_hi, flow - flow_hi, 1.0 - flag, pull_hi, pull - pull_hi]
            ):
                target[index : index + 1, here] = row[c : c + 1, :]
        rows[0:16, :] = target[...].astype(BF16)

    def multiply(rows, tilts):
        upper = rows[0 : 16 + features, :]
        gram_acc[...] += lax.dot_general(
            upper, rows[16:, :], CONTRACT_LAST, preferred_element_type=F32
        )
        jac_acc[...] += lax.dot_general(
            rows[...], tilts[0 : 5 * assets, :], CONTRACT_LAST, preferred_element_type=F32
        )
        jac_low[...] += lax.dot_general(
            upper, tilts[5 * assets :, :], CONTRACT_LAST, preferred_element_type=F32
        )

    def both(index, carry):
        pair(index).wait()
        multiply(rows_b, tilts_b)
        fill(2 * index, rows_a, tilts_a)
        multiply(rows_a, tilts_a)
        fill(2 * index + 1, rows_b, tilts_b)
        for copy in leave(index):
            copy.start()
        return carry

    lax.fori_loop(0, blocks // 2, both, 0)
    multiply(rows_b, tilts_b)

    def targets(t):
        pairs = [t[0:1] + t[1:2], t[2:3], t[3:4] + t[4:5], jnp.zeros((5, t.shape[1]), F32)]
        return jnp.concatenate(pairs, axis=0)

    mid = features // 2
    high = gram_acc[16:, 0:features]
    half = 0.5 * high + gram_acc[16:, features:]
    gram = half + half.T
    turned = pltpu.roll(gram[mid:, :], mid, 1)
    lanes = lax.broadcasted_iota(jnp.int32, (mid, features), 1)
    subs = lax.broadcasted_iota(jnp.int32, (mid, features), 0)
    gram_out[0:mid, :] = jnp.where(lanes >= subs, gram[0:mid, :], turned)
    corner = jnp.sum(jnp.where(lanes == subs, turned, 0.0), axis=0, keepdims=True)
    aims = targets(gram_acc[0:16, 0:features] + gram_acc[0:16, features:])
    rank = lax.broadcasted_iota(jnp.int32, (8, features), 0)
    gram_out[mid:, :] = jnp.where(rank == 3, jnp.broadcast_to(corner, (8, features)), aims)
    full = jac_acc[16 : 16 + features, :] + jac_acc[16 + features :, :] + jac_low[16:, :]
    aims = targets(jac_acc[0:16, :] + jac_low[0:16, :])
    jac[0:features, :] = full[:, 0:features]
    jac[features : features + assets, :] = jnp.concatenate(
        [full[assets * g : assets * (g + 1), features:] for g in range(4)], axis=1
    )
    jac[features + assets : features + assets + 8, :] = aims[:, 0:features]
    jac[features + assets + 8 :, :] = jnp.concatenate(
        [aims[:, features:], jnp.zeros((8, features - assets), F32)], axis=1
    )
    mine, other = halves(jac_keep.shape[0])
    jac_keep[...] = jac[mine, :]
    jac_give[...] = jac[other, :]
    for index in range(blocks // 2):
        for copy in leave(index):
            copy.wait()


def lane(block, index):
    return jnp.broadcast_to(block[:, index : index + 1], block.shape)


def solve_kernel(packed, out, spread):
    features = packed.shape[1]
    blocks = features // 8
    mid = features // 2
    lanes = lax.broadcasted_iota(jnp.int32, (mid, features), 1)
    subs = lax.broadcasted_iota(jnp.int32, (mid, features), 0)
    upper = packed[0:mid, :]
    aims = packed[mid:, :]
    corner = jnp.broadcast_to(aims[3:4], (mid, features))
    lower = jnp.where(lanes < subs, upper, jnp.where(lanes == subs, 0.5 * corner, 0.0))
    half = jnp.concatenate(
        [
            jnp.where(lanes == subs, 0.5 * upper, jnp.where(lanes > subs, upper, 0.0)),
            pltpu.roll(lower, mid, 1),
        ],
        axis=0,
    )
    gram = half + half.T
    lanes = lax.broadcasted_iota(jnp.int32, (8, features), 1)
    subs = lax.broadcasted_iota(jnp.int32, (8, features), 0)
    mat = [gram[8 * v : 8 * v + 8, :] for v in range(blocks)] + [aims]
    for k in range(blocks):
        base = 8 * k
        head = mat[k]
        diag = {}
        for j in range(8):
            col = lane(head, base + j)
            spread[0, j] = col
            for i in range(j + 1):
                diag[i, j] = jnp.broadcast_to(spread[0, j, i : i + 1, :], (8, features))
        inside = (lanes >= base) & (lanes < base + 8)
        spread[1, 0] = jnp.where(inside, jnp.where(lanes == base + subs, -1.0, 0.0), head)
        work = [jnp.broadcast_to(spread[1, 0, i : i + 1, :], (8, features)) for i in range(8)]
        inverse, low = [], {}
        for p in range(8):
            inv = 1.0 / diag[p, p]
            inverse.append(inv)
            for j in range(p + 1, 8):
                low[p, j] = diag[p, j] * inv
            for i in range(p + 1, 8):
                for j in range(i, 8):
                    diag[i, j] = diag[i, j] - low[p, i] * diag[p, j]
                work[i] = work[i] - low[p, i] * work[p]
        for i in reversed(range(8)):
            value = work[i] * inverse[i]
            for j in range(i + 1, 8):
                value = value - low[i, j] * work[j]
            work[i] = value
        for v in range(k + 1, blocks + 1):
            new = jnp.where(inside, 0.0, mat[v])
            for c in range(8):
                new = new - lane(mat[v], base + c) * work[c]
            mat[v] = new
    kept = jnp.broadcast_to(aims[2:3], (8, features))
    out[...] = jnp.where(subs == 3, kept, mat[blocks])


def adjoint_kernel(
    assets, width,
    solved, jac_mine, jac_other, spot, vol, weights, cash, taken,
    value_in, pull_in, scaled_in, bounded_in,
    value_out, flow_out, greeks_out, cot_out,
    coef, part, line, tangents, cot, jac, sent,
):
    features = 4 * assets
    paths = scaled_in.shape[1]
    chunks = width // LANES
    turned = solved[...].T
    spread = column(vol[...] * root_time, assets)
    base = column(spot[...], assets)
    weight = column(weights[...], assets)
    total = jnp.sum(weights[...] * spot[...], axis=1, keepdims=True)
    offsets = []
    for which in range(2):
        parts = [
            jnp.broadcast_to(turned[assets * g : assets * (g + 1), which : which + 1], (assets, LANES))
            for g in range(4)
        ]
        for g in range(4):
            coef[5 * which + g] = parts[g]
        coef[5 * which + 4] = pltpu.roll(parts[2], 1, 0)
        offsets.append(jnp.sum(parts[1], axis=0, keepdims=True))
    coef[10] = 1.0 / (base * spread)
    coef[11] = weight / jnp.broadcast_to(total, (assets, LANES))

    def leave(index):
        at = pl.ds(pl.multiple_of(index * (2 * width), 2 * width), 2 * width)
        return pltpu.make_async_copy(cot.at[:, at], cot_out.at[:, at], sent.at[index])

    def block(index, slot):
        for c in range(chunks):
            at = pl.ds(pl.multiple_of(index * width, width) + c * LANES, LANES)
            here = pl.ds(c * LANES, LANES)
            scaled = scaled_in[:, at]
            bounded = bounded_in[:, at]
            after = pltpu.roll(scaled, assets - 1, 0)
            before = pltpu.roll(scaled, 1, 0)
            curve = 1.0 - bounded * bounded
            for which in range(2):
                k = 5 * which
                bend = coef[k + 1] * scaled
                inner = coef[k] + bend + coef[k + 2] * after
                terms = scaled * inner + coef[k + 3] * bounded
                part[slot, which, 8 * c : 8 * c + 8, :] = sum(
                    terms[8 * g : 8 * g + 8] for g in range(assets // 8)
                )
                tangents[slot, which, :, here] = (
                    inner + bend + coef[k + 4] * before + coef[k + 3] * curve
                )
        at = pl.ds(pl.multiple_of(index * chunks, chunks), chunks)
        fitted = [
            sum(part[slot, which, pl.ds(i, chunks, stride=8), :] for i in range(8)) - offsets[which]
            for which in range(2)
        ]
        rest = 1.0 - taken[at, :].astype(F32)
        value_out[at, :] = value_in[at, :] + rest * fitted[0]
        flow_out[at, :] = fitted[1]
        line[slot, 0] = cash[at, :] - fitted[0]
        line[slot, 1] = rest - fitted[1]
        line[slot, 2] = pull_in[at, :]
        for c in range(chunks):
            at = pl.ds(pl.multiple_of(index * width, width) + c * LANES, LANES)
            here = pl.ds(c * LANES, LANES)
            miss, gap, pull = (
                jnp.broadcast_to(line[slot, i, c : c + 1, :], (assets, LANES)) for i in range(3)
            )
            cot[:, at] = (
                miss * tangents[slot, 1, :, here] + gap * tangents[slot, 0, :, here]
            ) * coef[10] + pull * coef[11]

    def both(index, carry):
        block(2 * index, 0)
        block(2 * index + 1, 1)
        leave(index).start()
        return carry

    lax.fori_loop(0, paths // (2 * width), both, 0)

    mine, other = halves(jac_mine.shape[0])
    jac[mine, :] = jac_mine[...]
    jac[other, :] = jac_other[...]
    regression, multiplier = solved[0:1, :], solved[1:2, :]
    group = lax.broadcasted_iota(jnp.int32, (assets, LANES), 1) // assets

    def against(which):
        main = jnp.sum(jac[0:features, :] * turned[:, which : which + 1], axis=0, keepdims=True)
        packed = jnp.zeros((assets, LANES), F32)
        for g in range(4):
            part = turned[assets * g : assets * (g + 1), which : which + 1]
            packed = jnp.where(group == g, jnp.broadcast_to(part, (assets, LANES)), packed)
        side = jnp.sum(jac[features : features + assets, :] * packed, axis=0, keepdims=True)
        side = side + pltpu.roll(side, 2 * assets, 1)
        side = side + pltpu.roll(side, assets, 1)
        return main, side

    aims = features + assets
    main_r, side_r = against(0)
    main_m, side_m = against(1)
    miss, gap = jac[aims : aims + 1, :] - main_r, jac[aims + 1 : aims + 2, :] - main_m
    miss_side = jac[aims + 8 : aims + 9, :] - side_r
    gap_side = jac[aims + 9 : aims + 10, :] - side_m
    lanes = lax.broadcasted_iota(jnp.int32, (1, LANES), 1)
    double = jnp.where((lanes >= assets) & (lanes < 2 * assets), 2.0, 1.0)
    total = double * (multiplier * miss + regression * gap)
    total = total + pltpu.roll(total, 2 * assets, 1)
    total = total + pltpu.roll(total, assets, 1)

    def earlier(row):
        moved = pltpu.roll(row, features - 2 * assets + 1, 1)
        wrapped = pltpu.roll(row, features - 3 * assets + 1, 1)
        return jnp.where(lanes == 0, wrapped, moved)

    total = total + earlier(multiplier) * miss_side + earlier(regression) * gap_side
    vega = total[:, 0:assets] / vol[...]
    pulled_slope = jac[aims + 2 : aims + 3, 0:assets]
    pulled_scaled = solved[3:4, 0:assets]
    pulled = solved[3:4, features - 1 : features]
    value = weights[...] * spot[...]
    whole = jnp.sum(value, axis=1, keepdims=True)
    growth = pulled + vol[...] * root_time * pulled_scaled
    mean = jnp.sum(value * growth, axis=1, keepdims=True) / whole
    delta = weights[...] / whole * (growth - mean)
    vega = vega + value * root_time / whole * (pulled_slope + pulled_scaled)
    greeks_out[...] = jnp.concatenate([delta, vega], axis=0)
    for index in range(paths // (2 * width)):
        leave(index).wait()


def swap(value, mask):
    count = math.prod(lax.axis_size(axis) for axis in AXES)
    return lax.ppermute(value, AXES, [(i, i ^ mask) for i in range(count)])


def gather_sum(value, masks):
    combos = [0]
    for mask in masks:
        combos = combos + [c ^ mask for c in combos]
    terms = [value] + [swap(value, c) for c in combos[1:]]
    while len(terms) > 1:
        terms = [a + b for a, b in zip(terms[::2], terms[1::2])]
    return terms[0]


def per_device(normals, spot, vol, weights, cash, taken):
    assets, paths = normals.shape
    features = 4 * assets
    path_total = paths * lax.axis_size("grp") * lax.axis_size("path")
    spot, vol, weights = (a.reshape(1, assets) for a in (spot, vol, weights))
    params = pltpu.CompilerParams(vmem_limit_bytes=16 * 1024 * 1024)
    big = jax.ShapeDtypeStruct((assets, paths), F32)
    jac_rows = features + assets + 16
    half = jax.ShapeDtypeStruct((jac_rows // 2, features), F32)
    compact = (paths // LANES, LANES)
    block = 8 * LANES
    remote = pl.BlockSpec(memory_space=pltpu.HBM)
    local = pl.BlockSpec(memory_space=pltpu.VMEM)
    short = jax.ShapeDtypeStruct(compact, F32)
    buffers = [
        pltpu.VMEM((16 + 2 * features, block), BF16),
        pltpu.VMEM((10 * assets, block), BF16),
    ]
    scaled, bounded, value, pull, gram, jac_keep, jac_give = pl.pallas_call(
        functools.partial(sums_kernel, assets, block),
        in_specs=[remote] * 6,
        out_specs=[remote] * 2 + [local] * 5,
        out_shape=[
            big, big, short, short,
            jax.ShapeDtypeStruct((features // 2 + 8, features), F32),
            half, half,
        ],
        scratch_shapes=[
            pltpu.VMEM((8, assets), F32),
            pltpu.VMEM(compact, F32),
            pltpu.VMEM(compact, jnp.int32),
            pltpu.VMEM((assets, paths), F32),
            pltpu.VMEM((4, assets, LANES), F32),
            pltpu.VMEM((64, LANES), F32),
            pltpu.VMEM((16, block), F32),
            pltpu.VMEM((assets, paths), F32),
            pltpu.VMEM((assets, paths), F32),
            *buffers, *buffers,
            pltpu.VMEM((16 + features, 2 * features), F32),
            pltpu.VMEM((16 + 2 * features, 5 * assets), F32),
            pltpu.VMEM((16 + features, 5 * assets), F32),
            pltpu.VMEM((jac_rows, features), F32),
            pltpu.SemaphoreType.DMA((5 + paths // (2 * block),)),
            pltpu.SemaphoreType.DMA((2, paths // (2 * block))),
        ],
        compiler_params=pltpu.CompilerParams(vmem_limit_bytes=60 * 1024 * 1024),
        name="sums",
    )(spot, vol, weights, cash.reshape(compact), taken.reshape(compact), normals)
    sizes = [lax.axis_size(axis) for axis in AXES]
    masks = [1 << bit for bit in range(math.prod(sizes).bit_length() - 1)]
    assert math.prod(sizes) == 1 << len(masks)
    scale = 1.0 / path_total
    gram = lax.optimization_barrier(gram * scale) + swap(gram, masks[0]) * scale
    jac_mine = lax.optimization_barrier(jac_keep * scale) + swap(jac_give, masks[0]) * scale
    packed = jnp.concatenate([gram, jac_mine], axis=0)
    later = masks[2:] + masks[1:2]
    for index in range(0, len(later), 2):
        packed = gather_sum(packed, later[index : index + 2])
    gram, jac_mine = packed[: gram.shape[0]], packed[gram.shape[0] :]
    jac_other = swap(jac_mine, masks[0])
    solved = pl.pallas_call(
        solve_kernel,
        out_shape=jax.ShapeDtypeStruct((8, features), F32),
        scratch_shapes=[pltpu.VMEM((2, 8, 8, features), F32)],
        compiler_params=params,
        cost_estimate=pl.CostEstimate(
            flops=4 * 10**9, bytes_accessed=15 * 10**6, transcendentals=features
        ),
        name="solve",
    )(gram)
    value, flow, greeks, cot = pl.pallas_call(
        functools.partial(adjoint_kernel, assets, block),
        in_specs=[local] * 12,
        out_specs=[local] * 3 + [remote],
        out_shape=[short, short, jax.ShapeDtypeStruct((2, assets), F32), big],
        scratch_shapes=[
            pltpu.VMEM((12, assets, LANES), F32),
            pltpu.VMEM((2, 2, 64, LANES), F32),
            pltpu.VMEM((2, 3, 8, LANES), F32),
            pltpu.VMEM((2, 2, assets, block), F32),
            pltpu.VMEM((assets, paths), F32),
            pltpu.VMEM((jac_rows, features), F32),
            pltpu.SemaphoreType.DMA((paths // (2 * block),)),
        ],
        compiler_params=params,
        name="adjoint",
    )(
        solved, jac_mine, jac_other, spot, vol, weights, cash.reshape(compact), taken.reshape(compact),
        value, pull, scaled, bounded,
    )
    return value.reshape(paths), cot, flow.reshape(paths), greeks


def solution(mesh):
    in_specs = (P(None, ("grp", "path")), P(), P(), P(), P(("grp", "path")), P(("grp", "path")))
    out_specs = (P(("grp", "path")), P(None, ("grp", "path")), P(("grp", "path")), P())
    return jax.shard_map(
        per_device, mesh=mesh, in_specs=in_specs, out_specs=out_specs, check_vma=False
    )
```

```python
import functools
import math

import jax
import jax.numpy as jnp
from jax import lax
from jax.experimental import pallas as pl
from jax.experimental.pallas import tpu as pltpu
from jax.sharding import PartitionSpec as P

root_time = math.sqrt(0.5)
notional = 20.0
soft_width = 0.02
LANES = 128
F32 = jnp.float32
BF16 = jnp.bfloat16
AXES = ("grp", "path")
CONTRACT_LAST = (((1,), (1,)), ((), ()))


def column(row, count):
    rows = lax.broadcasted_iota(jnp.int32, (count, count), 0)
    cols = lax.broadcasted_iota(jnp.int32, (count, count), 1)
    wide = jnp.broadcast_to(row, (count, count))
    picked = jnp.sum(jnp.where(rows == cols, wide, 0.0), axis=1, keepdims=True)
    return jnp.broadcast_to(picked, (count, LANES))


def split(x):
    hi = x.astype(BF16)
    lo = (x - hi.astype(F32)).astype(BF16)
    return hi, lo


def halves(rows):
    odd = lax.axis_index("path") & 1
    at = lambda index: pl.ds(pl.multiple_of(index * rows, 8), rows)
    return at(odd), at(1 - odd)


def sums_kernel(
    assets, width, spot, vol, weights, cash, taken, normals,
    scaled_out, bounded_out, value_out, pull_out, keep, give,
    small, flows, flags, draws, coef, part, target,
    scaled_all, bounded_all, slopes, rows_a, rows_b, acc, flow_acc, pull_acc, jac, sems, sent,
):
    features = 4 * assets
    paths = draws.shape[1]
    chunks = width // LANES
    blocks = paths // width
    copies = [
        pltpu.make_async_copy(spot, small.at[0:1, :], sems.at[0]),
        pltpu.make_async_copy(vol, small.at[1:2, :], sems.at[1]),
        pltpu.make_async_copy(weights, small.at[2:3, :], sems.at[2]),
        pltpu.make_async_copy(cash, flows, sems.at[3]),
        pltpu.make_async_copy(taken, flags, sems.at[4]),
    ]

    def pair(index):
        at = pl.ds(pl.multiple_of(index * (2 * width), 2 * width), 2 * width)
        return pltpu.make_async_copy(normals.at[:, at], draws.at[:, at], sems.at[5 + index])

    def leave(index):
        at = pl.ds(pl.multiple_of(index * (2 * width), 2 * width), 2 * width)
        return [
            pltpu.make_async_copy(scaled_all.at[:, at], scaled_out.at[:, at], sent.at[0, index]),
            pltpu.make_async_copy(bounded_all.at[:, at], bounded_out.at[:, at], sent.at[1, index]),
        ]

    for copy in copies[:3]:
        copy.start()
    for index in range(blocks // 2):
        pair(index).start()
        if index == 0:
            for copy in copies[3:]:
                copy.start()
    acc[...] = jnp.zeros_like(acc)
    flow_acc[...] = jnp.zeros_like(flow_acc)
    pull_acc[...] = jnp.zeros_like(pull_acc)
    rows_b[...] = jnp.zeros_like(rows_b)
    target[...] = jnp.zeros_like(target)
    for copy in copies[:3]:
        copy.wait()
    spread = column(small[1:2, :] * root_time, assets)
    value = small[2:3, :] * small[0:1, :]
    total = jnp.sum(value, axis=1, keepdims=True)
    coef[0] = spread
    coef[1] = 0.5 * spread * spread
    coef[2] = 1.0 / spread
    coef[3] = column(value, assets) / jnp.broadcast_to(total, (assets, LANES))
    for copy in copies[3:]:
        copy.wait()

    last = lax.broadcasted_iota(jnp.int32, (assets, LANES), 0) == assets - 1
    tail = lax.broadcasted_iota(jnp.int32, (16, LANES), 0) == 15
    aim, base, low = 10 * assets, 10 * assets + 16, 10 * assets + 16 + features

    def fill(block, rows, half):
        line = pl.ds(pl.multiple_of(block * chunks, chunks), chunks)
        flag = flags[line, :].astype(F32)
        flow = flows[line, :]
        rest = 1.0 - flag
        flow_sum = 0.0
        for c in range(half * chunks // 2, (half + 1) * chunks // 2):
            at = pl.ds(pl.multiple_of(block * width, width) + c * LANES, LANES)
            here = pl.ds(c * LANES, LANES)
            draw = draws[:, at]
            spread = coef[0]
            growth = jnp.exp(spread * draw - coef[1])
            weighted = growth * coef[3]
            part[8 * c : 8 * c + 8, :] = sum(weighted[8 * g : 8 * g + 8] for g in range(assets // 8))
            scaled = (growth - 1.0) * coef[2]
            bounded = jnp.where(last, 1.0, jnp.tanh(scaled))
            scaled_all[:, at] = scaled
            bounded_all[:, at] = bounded
            after = pltpu.roll(scaled, assets - 1, 0)
            before = pltpu.roll(scaled, 1, 0)
            basis = jnp.concatenate(
                [scaled, scaled * scaled - 1.0, scaled * after, bounded], axis=0
            )
            hi, lo = split(basis)
            rows[base : base + features, here] = hi
            rows[low : low + features - 16, here] = lo[: features - 16]
            ends = (basis - hi.astype(F32))[features - 16 :]
            kept = jnp.broadcast_to(rest[c : c + 1, :], (16, LANES))
            rows[low + features - 16 :, here] = jnp.where(tail, kept, ends).astype(BF16)
            slope = growth * (draw - spread) - scaled
            curve = 1.0 - bounded * bounded
            tilt = jnp.concatenate(
                [slope, slope * scaled, slope * after, slope * curve, slope * before], axis=0
            )
            hi, lo = split(tilt)
            rows[0 : 5 * assets, here] = hi
            rows[5 * assets : 10 * assets, here] = lo
            flow_sum = flow_sum + tilt * jnp.broadcast_to(flow[c : c + 1, :], tilt.shape)
            slopes[:, here] = slope
        flow_acc[...] += flow_sum
        if half == 0:
            return
        basket = sum(part[pl.ds(i, chunks, stride=8), :] for i in range(8))
        x = (basket - 1.0) * (1.0 / soft_width)
        decay = jnp.exp(-jnp.abs(x))
        reward = (notional * soft_width) * (jnp.maximum(x, 0.0) + jnp.log1p(decay))
        inverse = 1.0 / (1.0 + decay)
        sigmoid = jnp.where(x >= 0.0, inverse, decay * inverse)
        pull = notional * flag * sigmoid
        value_out[line, :] = flag * reward
        pull_out[line, :] = pull
        flow_hi = flow.astype(BF16).astype(F32)
        pull_hi = pull.astype(BF16).astype(F32)
        pull_sum = 0.0
        for c in range(chunks):
            here = pl.ds(c * LANES, LANES)
            for index, row in enumerate([flow_hi, flow - flow_hi, rest, pull_hi, pull - pull_hi]):
                target[index : index + 1, here] = row[c : c + 1, :]
            pull_sum = pull_sum + slopes[:, here] * jnp.broadcast_to(pull[c : c + 1, :], (assets, LANES))
        pull_acc[...] += pull_sum
        rows[aim : aim + 16, :] = target[...].astype(BF16)

    cut = 16 * ((low // 16 + 1) // 2)

    def multiply(rows, part):
        at = slice(0, cut) if part == 0 else slice(cut, low)
        acc[at, :] += lax.dot_general(
            rows[at, :], rows[base:, :], CONTRACT_LAST, preferred_element_type=F32
        )

    def both(index, carry):
        pair(index).wait()
        for part in range(2):
            multiply(rows_b, part)
            fill(2 * index, rows_a, part)
        for part in range(2):
            multiply(rows_a, part)
            fill(2 * index + 1, rows_b, part)
        for copy in leave(index):
            copy.start()
        return carry

    lax.fori_loop(0, blocks // 2, both, 0)
    multiply(rows_b, 0)
    multiply(rows_b, 1)

    mid = features // 2
    high = acc[base:low, 0:features]
    cross = acc[base:low, features:]
    edge = lax.broadcasted_iota(jnp.int32, (features, features), 1) == features - 1
    half = 0.5 * high + jnp.where(edge, 0.0, cross)
    gram = half + half.T
    turned = pltpu.roll(gram[mid:, :], mid, 1)
    lanes = lax.broadcasted_iota(jnp.int32, (mid, features), 1)
    subs = lax.broadcasted_iota(jnp.int32, (mid, features), 0)
    packed = jnp.where(lanes >= subs, gram[0:mid, :], turned)
    keep[0:mid, :] = packed
    give[0:mid, :] = packed
    corner = jnp.sum(jnp.where(lanes == subs, turned, 0.0), axis=0, keepdims=True)
    aimed = acc[aim : aim + 8, 0:features] + jnp.where(edge[0:8], 0.0, acc[aim : aim + 8, features:])
    aims = jnp.concatenate(
        [
            aimed[0:1] + aimed[1:2], aimed[2:3], aimed[3:4] + aimed[4:5],
            jnp.zeros((5, features), F32),
        ],
        axis=0,
    )
    rank = lax.broadcasted_iota(jnp.int32, (8, features), 0)
    packed = jnp.where(rank == 3, jnp.broadcast_to(corner, (8, features)), aims)
    keep[mid : mid + 8, :] = packed
    give[mid : mid + 8, :] = packed
    five = 5 * assets
    edge = edge[0:1]
    leaned = acc[0:five, features:]
    full = acc[0:five, 0:features] + acc[five:aim, 0:features] + jnp.where(edge, 0.0, leaned)
    rest = jnp.sum(jnp.where(edge, leaned + acc[five:aim, features:], 0.0), axis=1, keepdims=True)
    flow = jnp.sum(flow_acc[...], axis=1, keepdims=True)
    pull = jnp.sum(pull_acc[...], axis=1, keepdims=True)
    jac[0:five, :] = full
    slots = lax.broadcasted_iota(jnp.int32, (five, features), 1)
    pull = jnp.concatenate([pull, jnp.zeros((4 * assets, 1), F32)], axis=0)
    sides = jnp.where(
        slots == 0, flow, jnp.where(slots == 1, rest, jnp.where(slots == 2, pull, 0.0))
    ).T
    jac[five : five + 8, :] = sides[0:8, 0:features]
    jac[five + 8 : five + 16, :] = jnp.concatenate(
        [sides[0:8, features:], jnp.zeros((8, features - assets), F32)], axis=1
    )
    mine, other = halves(jac.shape[0] // 2)
    keep[mid + 8 :, :] = jac[mine, :]
    give[mid + 8 :, :] = jac[other, :]
    for index in range(blocks // 2):
        for copy in leave(index):
            copy.wait()


def lane(block, index):
    return jnp.broadcast_to(block[:, index : index + 1], block.shape)


def solve_kernel(packed, out, spread):
    features = packed.shape[1]
    blocks = features // 8
    mid = features // 2
    lanes = lax.broadcasted_iota(jnp.int32, (mid, features), 1)
    subs = lax.broadcasted_iota(jnp.int32, (mid, features), 0)
    upper = packed[0:mid, :]
    aims = packed[mid:, :]
    corner = jnp.broadcast_to(aims[3:4], (mid, features))
    lower = jnp.where(lanes < subs, upper, jnp.where(lanes == subs, 0.5 * corner, 0.0))
    half = jnp.concatenate(
        [
            jnp.where(lanes == subs, 0.5 * upper, jnp.where(lanes > subs, upper, 0.0)),
            pltpu.roll(lower, mid, 1),
        ],
        axis=0,
    )
    gram = half + half.T
    lanes = lax.broadcasted_iota(jnp.int32, (8, features), 1)
    subs = lax.broadcasted_iota(jnp.int32, (8, features), 0)
    mat = [gram[8 * v : 8 * v + 8, :] for v in range(blocks)] + [aims]
    for k in range(blocks):
        base = 8 * k
        head = mat[k]
        diag = {}
        for j in range(8):
            col = lane(head, base + j)
            spread[0, j] = col
            for i in range(j + 1):
                diag[i, j] = jnp.broadcast_to(spread[0, j, i : i + 1, :], (8, features))
        inside = (lanes >= base) & (lanes < base + 8)
        spread[1, 0] = jnp.where(inside, jnp.where(lanes == base + subs, -1.0, 0.0), head)
        work = [jnp.broadcast_to(spread[1, 0, i : i + 1, :], (8, features)) for i in range(8)]
        inverse, low = {}, {}
        for p in range(0, 8, 2):
            q = p + 1
            one, off, two = diag[p, p], diag[p, q], diag[q, q]
            inv = 1.0 / (one * two - off * off)
            inverse[p] = (two * inv, off * inv, one * inv)
            lift = {}
            for j in range(q + 1, 8):
                first, second = diag[p, j], diag[q, j]
                lift[j] = (two * first - off * second, one * second - off * first)
                low[p, j], low[q, j] = lift[j][0] * inv, lift[j][1] * inv
            for i in range(q + 1, 8):
                for j in range(i, 8):
                    drop = lift[i][0] * diag[p, j] + lift[i][1] * diag[q, j]
                    diag[i, j] = diag[i, j] - drop * inv
                work[i] = work[i] - (low[p, i] * work[p] + low[q, i] * work[q])
        for p in (6, 4, 2, 0):
            q = p + 1
            one, off, two = inverse[p]
            first = one * work[p] - off * work[q]
            second = two * work[q] - off * work[p]
            for j in reversed(range(q + 1, 8)):
                first = first - low[p, j] * work[j]
                second = second - low[q, j] * work[j]
            work[p], work[q] = first, second
        for v in range(k + 1, blocks + 1):
            new = jnp.where(inside, 0.0, mat[v])
            for c in reversed(range(8)):
                new = new - lane(mat[v], base + c) * work[c]
            mat[v] = new
    kept = jnp.broadcast_to(aims[2:3], (8, features))
    out[...] = jnp.where(subs == 3, kept, mat[blocks])


def adjoint_kernel(
    assets, width,
    solved, jac_mine, jac_other, spot, vol, weights, cash, taken,
    value_in, pull_in, scaled_in, bounded_in,
    value_out, flow_out, greeks_out, cot_out,
    coef, part, line, tangents, cot, jac, sent,
):
    features = 4 * assets
    paths = scaled_in.shape[1]
    chunks = width // LANES
    turned = solved[...].T
    spread = column(vol[...] * root_time, assets)
    base = column(spot[...], assets)
    weight = column(weights[...], assets)
    total = jnp.sum(weights[...] * spot[...], axis=1, keepdims=True)
    offsets = []
    for which in range(2):
        parts = [
            jnp.broadcast_to(turned[assets * g : assets * (g + 1), which : which + 1], (assets, LANES))
            for g in range(4)
        ]
        for g in range(4):
            coef[5 * which + g] = parts[g]
        coef[5 * which + 4] = pltpu.roll(parts[2], 1, 0)
        offsets.append(jnp.sum(parts[1], axis=0, keepdims=True))
    coef[10] = 1.0 / (base * spread)
    coef[11] = weight / jnp.broadcast_to(total, (assets, LANES))

    def leave(index):
        at = pl.ds(pl.multiple_of(index * (2 * width), 2 * width), 2 * width)
        return pltpu.make_async_copy(cot.at[:, at], cot_out.at[:, at], sent.at[index])

    def block(index, slot):
        for c in range(chunks):
            at = pl.ds(pl.multiple_of(index * width, width) + c * LANES, LANES)
            here = pl.ds(c * LANES, LANES)
            scaled = scaled_in[:, at]
            bounded = bounded_in[:, at]
            after = pltpu.roll(scaled, assets - 1, 0)
            before = pltpu.roll(scaled, 1, 0)
            curve = 1.0 - bounded * bounded
            for which in range(2):
                k = 5 * which
                bend = coef[k + 1] * scaled
                inner = coef[k] + bend + coef[k + 2] * after
                terms = scaled * inner + coef[k + 3] * bounded
                part[slot, which, 8 * c : 8 * c + 8, :] = sum(
                    terms[8 * g : 8 * g + 8] for g in range(assets // 8)
                )
                tangents[slot, which, :, here] = (
                    inner + bend + coef[k + 4] * before + coef[k + 3] * curve
                )
        at = pl.ds(pl.multiple_of(index * chunks, chunks), chunks)
        fitted = [
            sum(part[slot, which, pl.ds(i, chunks, stride=8), :] for i in range(8)) - offsets[which]
            for which in range(2)
        ]
        rest = 1.0 - taken[at, :].astype(F32)
        value_out[at, :] = value_in[at, :] + rest * fitted[0]
        flow_out[at, :] = fitted[1]
        line[slot, 0] = cash[at, :] - fitted[0]
        line[slot, 1] = rest - fitted[1]
        line[slot, 2] = pull_in[at, :]
        for c in range(chunks):
            at = pl.ds(pl.multiple_of(index * width, width) + c * LANES, LANES)
            here = pl.ds(c * LANES, LANES)
            miss, gap, pull = (
                jnp.broadcast_to(line[slot, i, c : c + 1, :], (assets, LANES)) for i in range(3)
            )
            cot[:, at] = (
                miss * tangents[slot, 1, :, here] + gap * tangents[slot, 0, :, here]
            ) * coef[10] + pull * coef[11]

    def both(index, carry):
        block(2 * index, 0)
        block(2 * index + 1, 1)
        leave(index).start()
        return carry

    lax.fori_loop(0, paths // (2 * width), both, 0)

    mine, other = halves(jac_mine.shape[0])
    jac[mine, :] = jac_mine[...]
    jac[other, :] = jac_other[...]
    regression, multiplier = solved[0:1, :], solved[1:2, :]
    aims = features + assets
    against = lax.dot_general(
        solved[...], jac[0:aims, :], CONTRACT_LAST,
        precision=lax.Precision.HIGHEST, preferred_element_type=F32,
    )
    miss = jac[aims : aims + 1, :] - against[0:1, 0:features]
    gap = jac[aims + 1 : aims + 2, :] - against[1:2, 0:features]
    miss_side = jac[aims + 8 : aims + 9, 0:assets] - against[0:1, features:]
    gap_side = jac[aims + 9 : aims + 10, 0:assets] - against[1:2, features:]
    lanes = lax.broadcasted_iota(jnp.int32, (1, LANES), 1)
    double = jnp.where((lanes >= assets) & (lanes < 2 * assets), 2.0, 1.0)
    total = double * (multiplier * miss + regression * gap)
    total = total + pltpu.roll(total, 2 * assets, 1)
    total = total + pltpu.roll(total, assets, 1)

    def earlier(row):
        moved = pltpu.roll(row, features - 2 * assets + 1, 1)
        wrapped = pltpu.roll(row, features - 3 * assets + 1, 1)
        return jnp.where(lanes == 0, wrapped, moved)

    side = earlier(multiplier)[:, 0:assets] * miss_side + earlier(regression)[:, 0:assets] * gap_side
    vega = (total[:, 0:assets] + side) / vol[...]
    pulled_slope = jac[aims + 2 : aims + 3, 0:assets]
    pulled_scaled = solved[3:4, 0:assets]
    pulled = solved[3:4, features - 1 : features]
    value = weights[...] * spot[...]
    whole = jnp.sum(value, axis=1, keepdims=True)
    growth = pulled + vol[...] * root_time * pulled_scaled
    mean = jnp.sum(value * growth, axis=1, keepdims=True) / whole
    delta = weights[...] / whole * (growth - mean)
    vega = vega + value * root_time / whole * (pulled_slope + pulled_scaled)
    greeks_out[...] = jnp.concatenate([delta, vega], axis=0)
    for index in range(paths // (2 * width)):
        leave(index).wait()


def swap(value, mask):
    count = math.prod(lax.axis_size(axis) for axis in AXES)
    return lax.ppermute(value, AXES, [(i, i ^ mask) for i in range(count)])


def gather_sum(value, masks):
    combos = [0]
    for mask in masks:
        combos = combos + [c ^ mask for c in combos]
    terms = [value] + [swap(value, c) for c in combos[1:]]
    while len(terms) > 1:
        terms = [a + b for a, b in zip(terms[::2], terms[1::2])]
    return terms[0]


def per_device(normals, spot, vol, weights, cash, taken):
    assets, paths = normals.shape
    features = 4 * assets
    path_total = paths * lax.axis_size("grp") * lax.axis_size("path")
    spot, vol, weights = (a.reshape(1, assets) for a in (spot, vol, weights))
    params = pltpu.CompilerParams(vmem_limit_bytes=16 * 1024 * 1024)
    big = jax.ShapeDtypeStruct((assets, paths), F32)
    jac_rows = features + assets + 16
    gram_rows = features // 2 + 8
    sent = jax.ShapeDtypeStruct((gram_rows + jac_rows // 2, features), F32)
    compact = (paths // LANES, LANES)
    block = 8 * LANES
    remote = pl.BlockSpec(memory_space=pltpu.HBM)
    local = pl.BlockSpec(memory_space=pltpu.VMEM)
    short = jax.ShapeDtypeStruct(compact, F32)
    rows = pltpu.VMEM((10 * assets + 16 + 2 * features, block), BF16)
    scaled, bounded, value, pull, keep, give = pl.pallas_call(
        functools.partial(sums_kernel, assets, block),
        in_specs=[remote] * 6,
        out_specs=[remote] * 2 + [local] * 4,
        out_shape=[
            big, big, short, short,
            sent, sent,
        ],
        scratch_shapes=[
            pltpu.VMEM((8, assets), F32),
            pltpu.VMEM(compact, F32),
            pltpu.VMEM(compact, jnp.int32),
            pltpu.VMEM((assets, paths), F32),
            pltpu.VMEM((4, assets, LANES), F32),
            pltpu.VMEM((64, LANES), F32),
            pltpu.VMEM((16, block), F32),
            pltpu.VMEM((assets, paths), F32),
            pltpu.VMEM((assets, paths), F32),
            pltpu.VMEM((assets, block), F32),
            rows, rows,
            pltpu.VMEM((10 * assets + 16 + features, 2 * features), F32),
            pltpu.VMEM((5 * assets, LANES), F32),
            pltpu.VMEM((assets, LANES), F32),
            pltpu.VMEM((jac_rows, features), F32),
            pltpu.SemaphoreType.DMA((5 + paths // (2 * block),)),
            pltpu.SemaphoreType.DMA((2, paths // (2 * block))),
        ],
        compiler_params=pltpu.CompilerParams(vmem_limit_bytes=60 * 1024 * 1024),
        name="sums",
    )(spot, vol, weights, cash.reshape(compact), taken.reshape(compact), normals)
    sizes = [lax.axis_size(axis) for axis in AXES]
    masks = [1 << bit for bit in range(math.prod(sizes).bit_length() - 1)]
    assert math.prod(sizes) == 1 << len(masks)
    scale = 1.0 / path_total
    packed = lax.optimization_barrier(keep * scale) + swap(give, masks[0]) * scale
    for group in [[masks[1], masks[-1]]] + [[mask] for mask in masks[2:-1]]:
        packed = gather_sum(packed, group)
    gram, jac_mine = packed[:gram_rows], packed[gram_rows:]
    jac_other = swap(jac_mine, masks[0])
    solved = pl.pallas_call(
        solve_kernel,
        out_shape=jax.ShapeDtypeStruct((8, features), F32),
        scratch_shapes=[pltpu.VMEM((2, 8, 8, features), F32)],
        compiler_params=params,
        cost_estimate=pl.CostEstimate(
            flops=4 * 10**9, bytes_accessed=15 * 10**6, transcendentals=features
        ),
        name="solve",
    )(gram)
    value, flow, greeks, cot = pl.pallas_call(
        functools.partial(adjoint_kernel, assets, block),
        in_specs=[local] * 12,
        out_specs=[local] * 3 + [remote],
        out_shape=[short, short, jax.ShapeDtypeStruct((2, assets), F32), big],
        scratch_shapes=[
            pltpu.VMEM((12, assets, LANES), F32),
            pltpu.VMEM((2, 2, 64, LANES), F32),
            pltpu.VMEM((2, 3, 8, LANES), F32),
            pltpu.VMEM((2, 2, assets, block), F32),
            pltpu.VMEM((assets, paths), F32),
            pltpu.VMEM((jac_rows, features), F32),
            pltpu.SemaphoreType.DMA((paths // (2 * block),)),
        ],
        compiler_params=params,
        name="adjoint",
    )(
        solved, jac_mine, jac_other, spot, vol, weights, cash.reshape(compact), taken.reshape(compact),
        value, pull, scaled, bounded,
    )
    return value.reshape(paths), cot, flow.reshape(paths), greeks


def solution(mesh):
    in_specs = (P(None, ("grp", "path")), P(), P(), P(), P(("grp", "path")), P(("grp", "path")))
    out_specs = (P(("grp", "path")), P(None, ("grp", "path")), P(("grp", "path")), P())
    return jax.shard_map(
        per_device, mesh=mesh, in_specs=in_specs, out_specs=out_specs, check_vma=False
    )
```

```python
import functools
import math

import jax
import jax.numpy as jnp
from jax import lax
from jax.experimental import pallas as pl
from jax.experimental.pallas import tpu as pltpu
from jax.sharding import PartitionSpec as P

root_time = math.sqrt(0.5)
notional = 20.0
soft_width = 0.02
LANES = 128
F32 = jnp.float32
BF16 = jnp.bfloat16
AXES = ("grp", "path")
CONTRACT_LAST = (((1,), (1,)), ((), ()))


def column(row, count):
    rows = lax.broadcasted_iota(jnp.int32, (count, count), 0)
    cols = lax.broadcasted_iota(jnp.int32, (count, count), 1)
    wide = jnp.broadcast_to(row, (count, count))
    picked = jnp.sum(jnp.where(rows == cols, wide, 0.0), axis=1, keepdims=True)
    return jnp.broadcast_to(picked, (count, LANES))


def split(x):
    hi = x.astype(BF16)
    lo = (x - hi.astype(F32)).astype(BF16)
    return hi, lo


def halves(rows):
    odd = lax.axis_index("path") & 1
    at = lambda index: pl.ds(pl.multiple_of(index * rows, 8), rows)
    return at(odd), at(1 - odd)


def sums_kernel(
    assets, width, spot, vol, weights, cash, taken, normals,
    scaled_out, bounded_out, value_out, pull_out, keep, give,
    small, flows, flags, draws, coef, part, target,
    scaled_all, bounded_all, slopes, rows_a, rows_b, acc, flow_acc, pull_acc, jac, sems, sent,
):
    features = 4 * assets
    paths = draws.shape[1]
    chunks = width // LANES
    blocks = paths // width
    copies = [
        pltpu.make_async_copy(spot, small.at[0:1, :], sems.at[0]),
        pltpu.make_async_copy(vol, small.at[1:2, :], sems.at[1]),
        pltpu.make_async_copy(weights, small.at[2:3, :], sems.at[2]),
        pltpu.make_async_copy(cash, flows, sems.at[3]),
        pltpu.make_async_copy(taken, flags, sems.at[4]),
    ]

    def pair(index):
        at = pl.ds(pl.multiple_of(index * (2 * width), 2 * width), 2 * width)
        return pltpu.make_async_copy(normals.at[:, at], draws.at[:, at], sems.at[5 + index])

    def leave(index):
        at = pl.ds(pl.multiple_of(index * (2 * width), 2 * width), 2 * width)
        return [
            pltpu.make_async_copy(scaled_all.at[:, at], scaled_out.at[:, at], sent.at[0, index]),
            pltpu.make_async_copy(bounded_all.at[:, at], bounded_out.at[:, at], sent.at[1, index]),
        ]

    for copy in copies[:3]:
        copy.start()
    for index in range(blocks // 2):
        pair(index).start()
        if index == 0:
            for copy in copies[3:]:
                copy.start()
    acc[...] = jnp.zeros_like(acc)
    flow_acc[...] = jnp.zeros_like(flow_acc)
    pull_acc[...] = jnp.zeros_like(pull_acc)
    rows_b[...] = jnp.zeros_like(rows_b)
    target[...] = jnp.zeros_like(target)
    for copy in copies[:3]:
        copy.wait()
    spread = column(small[1:2, :] * root_time, assets)
    value = small[2:3, :] * small[0:1, :]
    total = jnp.sum(value, axis=1, keepdims=True)
    coef[0] = spread
    coef[1] = 0.5 * spread * spread
    coef[2] = 1.0 / spread
    coef[3] = column(value, assets) / jnp.broadcast_to(total, (assets, LANES))
    for copy in copies[3:]:
        copy.wait()

    last = lax.broadcasted_iota(jnp.int32, (assets, LANES), 0) == assets - 1
    tail = lax.broadcasted_iota(jnp.int32, (16, LANES), 0) == 15
    aim, base, low = 10 * assets, 10 * assets + 16, 10 * assets + 16 + features

    def fill(block, rows, half):
        line = pl.ds(pl.multiple_of(block * chunks, chunks), chunks)
        flag = flags[line, :].astype(F32)
        flow = flows[line, :]
        rest = 1.0 - flag
        flow_sum = 0.0
        for c in range(half * chunks // 2, (half + 1) * chunks // 2):
            at = pl.ds(pl.multiple_of(block * width, width) + c * LANES, LANES)
            here = pl.ds(c * LANES, LANES)
            draw = draws[:, at]
            spread = coef[0]
            growth = jnp.exp(spread * draw - coef[1])
            weighted = growth * coef[3]
            part[8 * c : 8 * c + 8, :] = sum(weighted[8 * g : 8 * g + 8] for g in range(assets // 8))
            scaled = (growth - 1.0) * coef[2]
            bounded = jnp.where(last, 1.0, jnp.tanh(scaled))
            scaled_all[:, at] = scaled
            bounded_all[:, at] = bounded
            after = pltpu.roll(scaled, assets - 1, 0)
            before = pltpu.roll(scaled, 1, 0)
            basis = jnp.concatenate(
                [scaled, scaled * scaled - 1.0, scaled * after, bounded], axis=0
            )
            hi, lo = split(basis)
            rows[base : base + features, here] = hi
            rows[low : low + features - 16, here] = lo[: features - 16]
            ends = (basis - hi.astype(F32))[features - 16 :]
            kept = jnp.broadcast_to(rest[c : c + 1, :], (16, LANES))
            rows[low + features - 16 :, here] = jnp.where(tail, kept, ends).astype(BF16)
            slope = growth * (draw - spread) - scaled
            curve = 1.0 - bounded * bounded
            tilt = jnp.concatenate(
                [slope, slope * scaled, slope * after, slope * curve, slope * before], axis=0
            )
            hi, lo = split(tilt)
            rows[0 : 5 * assets, here] = hi
            rows[5 * assets : 10 * assets, here] = lo
            flow_sum = flow_sum + tilt * jnp.broadcast_to(flow[c : c + 1, :], tilt.shape)
            slopes[:, here] = slope
        flow_acc[...] += flow_sum
        if half == 0:
            return
        basket = sum(part[pl.ds(i, chunks, stride=8), :] for i in range(8))
        x = (basket - 1.0) * (1.0 / soft_width)
        decay = jnp.exp(-jnp.abs(x))
        reward = (notional * soft_width) * (jnp.maximum(x, 0.0) + jnp.log1p(decay))
        inverse = 1.0 / (1.0 + decay)
        sigmoid = jnp.where(x >= 0.0, inverse, decay * inverse)
        pull = notional * flag * sigmoid
        value_out[line, :] = flag * reward
        pull_out[line, :] = pull
        flow_hi = flow.astype(BF16).astype(F32)
        pull_hi = pull.astype(BF16).astype(F32)
        pull_sum = 0.0
        for c in range(chunks):
            here = pl.ds(c * LANES, LANES)
            for index, row in enumerate([flow_hi, flow - flow_hi, rest, pull_hi, pull - pull_hi]):
                target[index : index + 1, here] = row[c : c + 1, :]
            pull_sum = pull_sum + slopes[:, here] * jnp.broadcast_to(pull[c : c + 1, :], (assets, LANES))
        pull_acc[...] += pull_sum
        rows[aim : aim + 16, :] = target[...].astype(BF16)

    cut = 16 * ((low // 16 + 1) // 2)

    def multiply(rows, part):
        at = slice(0, cut) if part == 0 else slice(cut, low)
        acc[at, :] += lax.dot_general(
            rows[at, :], rows[base:, :], CONTRACT_LAST, preferred_element_type=F32
        )

    def both(index, carry):
        pair(index).wait()
        for part in range(2):
            multiply(rows_b, part)
            fill(2 * index, rows_a, part)
        for part in range(2):
            multiply(rows_a, part)
            fill(2 * index + 1, rows_b, part)
        for copy in leave(index):
            copy.start()
        return carry

    lax.fori_loop(0, blocks // 2, both, 0)
    multiply(rows_b, 0)
    multiply(rows_b, 1)

    mid = features // 2
    high = acc[base:low, 0:features]
    cross = acc[base:low, features:]
    edge = lax.broadcasted_iota(jnp.int32, (features, features), 1) == features - 1
    half = 0.5 * high + jnp.where(edge, 0.0, cross)
    gram = half + half.T
    turned = pltpu.roll(gram[mid:, :], mid, 1)
    lanes = lax.broadcasted_iota(jnp.int32, (mid, features), 1)
    subs = lax.broadcasted_iota(jnp.int32, (mid, features), 0)
    packed = jnp.where(lanes >= subs, gram[0:mid, :], turned)
    keep[0:mid, :] = packed
    give[0:mid, :] = packed
    corner = jnp.sum(jnp.where(lanes == subs, turned, 0.0), axis=0, keepdims=True)
    aimed = acc[aim : aim + 8, 0:features] + jnp.where(edge[0:8], 0.0, acc[aim : aim + 8, features:])
    aims = jnp.concatenate(
        [
            aimed[0:1] + aimed[1:2], aimed[2:3], aimed[3:4] + aimed[4:5],
            jnp.zeros((5, features), F32),
        ],
        axis=0,
    )
    rank = lax.broadcasted_iota(jnp.int32, (8, features), 0)
    packed = jnp.where(rank == 3, jnp.broadcast_to(corner, (8, features)), aims)
    keep[mid : mid + 8, :] = packed
    give[mid : mid + 8, :] = packed
    five = 5 * assets
    edge = edge[0:1]
    leaned = acc[0:five, features:]
    full = acc[0:five, 0:features] + acc[five:aim, 0:features] + jnp.where(edge, 0.0, leaned)
    rest = jnp.sum(jnp.where(edge, leaned + acc[five:aim, features:], 0.0), axis=1, keepdims=True)
    flow = jnp.sum(flow_acc[...], axis=1, keepdims=True)
    pull = jnp.sum(pull_acc[...], axis=1, keepdims=True)
    jac[0:five, :] = full
    slots = lax.broadcasted_iota(jnp.int32, (five, features), 1)
    pull = jnp.concatenate([pull, jnp.zeros((4 * assets, 1), F32)], axis=0)
    sides = jnp.where(
        slots == 0, flow, jnp.where(slots == 1, rest, jnp.where(slots == 2, pull, 0.0))
    ).T
    jac[five : five + 8, :] = sides[0:8, 0:features]
    jac[five + 8 : five + 16, :] = jnp.concatenate(
        [sides[0:8, features:], jnp.zeros((8, features - assets), F32)], axis=1
    )
    mine, other = halves(jac.shape[0] // 2)
    keep[mid + 8 :, :] = jac[mine, :]
    give[mid + 8 :, :] = jac[other, :]
    for index in range(blocks // 2):
        for copy in leave(index):
            copy.wait()


def lane(block, index):
    return jnp.broadcast_to(block[:, index : index + 1], block.shape)


def solve_kernel(packed, out, spread):
    features = packed.shape[1]
    blocks = features // 8
    mid = features // 2
    lanes = lax.broadcasted_iota(jnp.int32, (mid, features), 1)
    subs = lax.broadcasted_iota(jnp.int32, (mid, features), 0)
    upper = packed[0:mid, :]
    aims = packed[mid:, :]
    corner = jnp.broadcast_to(aims[3:4], (mid, features))
    lower = jnp.where(lanes < subs, upper, jnp.where(lanes == subs, 0.5 * corner, 0.0))
    half = jnp.concatenate(
        [
            jnp.where(lanes == subs, 0.5 * upper, jnp.where(lanes > subs, upper, 0.0)),
            pltpu.roll(lower, mid, 1),
        ],
        axis=0,
    )
    gram = half + half.T
    lanes = lax.broadcasted_iota(jnp.int32, (8, features), 1)
    subs = lax.broadcasted_iota(jnp.int32, (8, features), 0)
    mat = [gram[8 * v : 8 * v + 8, :] for v in range(blocks)] + [aims]
    for k in range(blocks):
        base = 8 * k
        head = mat[k]
        diag = {}
        for j in range(8):
            col = lane(head, base + j)
            spread[0, j] = col
            for i in range(j + 1):
                diag[i, j] = jnp.broadcast_to(spread[0, j, i : i + 1, :], (8, features))
        inside = (lanes >= base) & (lanes < base + 8)
        spread[1, 0] = jnp.where(inside, jnp.where(lanes == base + subs, -1.0, 0.0), head)
        work = [jnp.broadcast_to(spread[1, 0, i : i + 1, :], (8, features)) for i in range(8)]
        inverse, low = {}, {}
        for p in range(0, 8, 2):
            q = p + 1
            one, off, two = diag[p, p], diag[p, q], diag[q, q]
            inv = 1.0 / (one * two - off * off)
            inverse[p] = (two * inv, off * inv, one * inv)
            lift = {}
            for j in range(q + 1, 8):
                first, second = diag[p, j], diag[q, j]
                lift[j] = (two * first - off * second, one * second - off * first)
                low[p, j], low[q, j] = lift[j][0] * inv, lift[j][1] * inv
            for i in range(q + 1, 8):
                for j in range(i, 8):
                    drop = lift[i][0] * diag[p, j] + lift[i][1] * diag[q, j]
                    diag[i, j] = diag[i, j] - drop * inv
                work[i] = work[i] - (low[p, i] * work[p] + low[q, i] * work[q])
        for p in (6, 4, 2, 0):
            q = p + 1
            one, off, two = inverse[p]
            first = one * work[p] - off * work[q]
            second = two * work[q] - off * work[p]
            for j in reversed(range(q + 1, 8)):
                first = first - low[p, j] * work[j]
                second = second - low[q, j] * work[j]
            work[p], work[q] = first, second
        for v in range(k + 1, blocks + 1):
            new = jnp.where(inside, 0.0, mat[v])
            for c in reversed(range(8)):
                new = new - lane(mat[v], base + c) * work[c]
            mat[v] = new
    kept = jnp.broadcast_to(aims[2:3], (8, features))
    out[...] = jnp.where(subs == 3, kept, mat[blocks])


def adjoint_kernel(
    assets, width,
    solved, jac_mine, jac_other, spot, vol, weights, cash, taken,
    value_in, pull_in, scaled_in, bounded_in,
    value_out, flow_out, greeks_out, cot_out,
    coef, part, line, tangents, cot, jac, sent,
):
    features = 4 * assets
    paths = scaled_in.shape[1]
    chunks = width // LANES
    turned = solved[...].T
    spread = column(vol[...] * root_time, assets)
    base = column(spot[...], assets)
    weight = column(weights[...], assets)
    total = jnp.sum(weights[...] * spot[...], axis=1, keepdims=True)
    offsets = []
    for which in range(2):
        parts = [
            jnp.broadcast_to(turned[assets * g : assets * (g + 1), which : which + 1], (assets, LANES))
            for g in range(4)
        ]
        for g in range(4):
            coef[5 * which + g] = parts[g]
        coef[5 * which + 4] = pltpu.roll(parts[2], 1, 0)
        offsets.append(jnp.sum(parts[1], axis=0, keepdims=True))
    coef[10] = 1.0 / (base * spread)
    coef[11] = weight / jnp.broadcast_to(total, (assets, LANES))

    def leave(index):
        at = pl.ds(pl.multiple_of(index * (2 * width), 2 * width), 2 * width)
        return pltpu.make_async_copy(cot.at[:, at], cot_out.at[:, at], sent.at[index])

    def block(index, slot):
        for c in range(chunks):
            at = pl.ds(pl.multiple_of(index * width, width) + c * LANES, LANES)
            here = pl.ds(c * LANES, LANES)
            scaled = scaled_in[:, at]
            bounded = bounded_in[:, at]
            after = pltpu.roll(scaled, assets - 1, 0)
            before = pltpu.roll(scaled, 1, 0)
            curve = 1.0 - bounded * bounded
            for which in range(2):
                k = 5 * which
                bend = coef[k + 1] * scaled
                inner = coef[k] + bend + coef[k + 2] * after
                terms = scaled * inner + coef[k + 3] * bounded
                part[slot, which, 8 * c : 8 * c + 8, :] = sum(
                    terms[8 * g : 8 * g + 8] for g in range(assets // 8)
                )
                tangents[slot, which, :, here] = (
                    inner + bend + coef[k + 4] * before + coef[k + 3] * curve
                )
        at = pl.ds(pl.multiple_of(index * chunks, chunks), chunks)
        fitted = [
            sum(part[slot, which, pl.ds(i, chunks, stride=8), :] for i in range(8)) - offsets[which]
            for which in range(2)
        ]
        rest = 1.0 - taken[at, :].astype(F32)
        value_out[at, :] = value_in[at, :] + rest * fitted[0]
        flow_out[at, :] = fitted[1]
        line[slot, 0] = cash[at, :] - fitted[0]
        line[slot, 1] = rest - fitted[1]
        line[slot, 2] = pull_in[at, :]
        for c in range(chunks):
            at = pl.ds(pl.multiple_of(index * width, width) + c * LANES, LANES)
            here = pl.ds(c * LANES, LANES)
            miss, gap, pull = (
                jnp.broadcast_to(line[slot, i, c : c + 1, :], (assets, LANES)) for i in range(3)
            )
            cot[:, at] = (
                miss * tangents[slot, 1, :, here] + gap * tangents[slot, 0, :, here]
            ) * coef[10] + pull * coef[11]

    def both(index, carry):
        block(2 * index, 0)
        block(2 * index + 1, 1)
        leave(index).start()
        return carry

    lax.fori_loop(0, paths // (2 * width), both, 0)

    mine, other = halves(jac_mine.shape[0])
    jac[mine, :] = jac_mine[...]
    jac[other, :] = jac_other[...]
    regression, multiplier = solved[0:1, :], solved[1:2, :]
    aims = features + assets
    against = lax.dot_general(
        solved[...], jac[0:aims, :], CONTRACT_LAST,
        precision=lax.Precision.HIGHEST, preferred_element_type=F32,
    )
    miss = jac[aims : aims + 1, :] - against[0:1, 0:features]
    gap = jac[aims + 1 : aims + 2, :] - against[1:2, 0:features]
    miss_side = jac[aims + 8 : aims + 9, 0:assets] - against[0:1, features:]
    gap_side = jac[aims + 9 : aims + 10, 0:assets] - against[1:2, features:]
    lanes = lax.broadcasted_iota(jnp.int32, (1, LANES), 1)
    double = jnp.where((lanes >= assets) & (lanes < 2 * assets), 2.0, 1.0)
    total = double * (multiplier * miss + regression * gap)
    total = total + pltpu.roll(total, 2 * assets, 1)
    total = total + pltpu.roll(total, assets, 1)

    def earlier(row):
        moved = pltpu.roll(row, features - 2 * assets + 1, 1)
        wrapped = pltpu.roll(row, features - 3 * assets + 1, 1)
        return jnp.where(lanes == 0, wrapped, moved)

    side = earlier(multiplier)[:, 0:assets] * miss_side + earlier(regression)[:, 0:assets] * gap_side
    vega = (total[:, 0:assets] + side) / vol[...]
    pulled_slope = jac[aims + 2 : aims + 3, 0:assets]
    pulled_scaled = solved[3:4, 0:assets]
    pulled = solved[3:4, features - 1 : features]
    value = weights[...] * spot[...]
    whole = jnp.sum(value, axis=1, keepdims=True)
    growth = pulled + vol[...] * root_time * pulled_scaled
    mean = jnp.sum(value * growth, axis=1, keepdims=True) / whole
    delta = weights[...] / whole * (growth - mean)
    vega = vega + value * root_time / whole * (pulled_slope + pulled_scaled)
    greeks_out[...] = jnp.concatenate([delta, vega], axis=0)
    for index in range(paths // (2 * width)):
        leave(index).wait()


def swap(value, mask):
    count = math.prod(lax.axis_size(axis) for axis in AXES)
    return lax.ppermute(value, AXES, [(i, i ^ mask) for i in range(count)])


def gather_sum(value, masks):
    combos = [0]
    for mask in masks:
        combos = combos + [c ^ mask for c in combos]
    terms = [value] + [swap(value, c) for c in combos[1:]]
    while len(terms) > 1:
        terms = [a + b for a, b in zip(terms[::2], terms[1::2])]
    return terms[0]


def per_device(normals, spot, vol, weights, cash, taken):
    assets, paths = normals.shape
    features = 4 * assets
    path_total = paths * lax.axis_size("grp") * lax.axis_size("path")
    spot, vol, weights = (a.reshape(1, assets) for a in (spot, vol, weights))
    params = pltpu.CompilerParams(vmem_limit_bytes=16 * 1024 * 1024)
    big = jax.ShapeDtypeStruct((assets, paths), F32)
    jac_rows = features + assets + 16
    gram_rows = features // 2 + 8
    sent = jax.ShapeDtypeStruct((gram_rows + jac_rows // 2, features), F32)
    compact = (paths // LANES, LANES)
    block = 8 * LANES
    remote = pl.BlockSpec(memory_space=pltpu.HBM)
    local = pl.BlockSpec(memory_space=pltpu.VMEM)
    short = jax.ShapeDtypeStruct(compact, F32)
    wide = 16 * LANES
    rows = pltpu.VMEM((10 * assets + 16 + 2 * features, wide), BF16)
    scaled, bounded, value, pull, keep, give = pl.pallas_call(
        functools.partial(sums_kernel, assets, wide),
        in_specs=[remote] * 6,
        out_specs=[remote] * 2 + [local] * 4,
        out_shape=[
            big, big, short, short,
            sent, sent,
        ],
        scratch_shapes=[
            pltpu.VMEM((8, assets), F32),
            pltpu.VMEM(compact, F32),
            pltpu.VMEM(compact, jnp.int32),
            pltpu.VMEM((assets, paths), F32),
            pltpu.VMEM((4, assets, LANES), F32),
            pltpu.VMEM((wide // 16, LANES), F32),
            pltpu.VMEM((16, wide), F32),
            pltpu.VMEM((assets, paths), F32),
            pltpu.VMEM((assets, paths), F32),
            pltpu.VMEM((assets, wide), F32),
            rows, rows,
            pltpu.VMEM((10 * assets + 16 + features, 2 * features), F32),
            pltpu.VMEM((5 * assets, LANES), F32),
            pltpu.VMEM((assets, LANES), F32),
            pltpu.VMEM((jac_rows, features), F32),
            pltpu.SemaphoreType.DMA((5 + paths // (2 * wide),)),
            pltpu.SemaphoreType.DMA((2, paths // (2 * wide))),
        ],
        compiler_params=pltpu.CompilerParams(vmem_limit_bytes=60 * 1024 * 1024),
        name="sums",
    )(spot, vol, weights, cash.reshape(compact), taken.reshape(compact), normals)
    sizes = [lax.axis_size(axis) for axis in AXES]
    masks = [1 << bit for bit in range(math.prod(sizes).bit_length() - 1)]
    assert math.prod(sizes) == 1 << len(masks)
    scale = 1.0 / path_total
    packed = lax.optimization_barrier(keep * scale) + swap(give, masks[0]) * scale
    for group in [[masks[1], masks[-1]]] + [[mask] for mask in masks[2:-1]]:
        packed = gather_sum(packed, group)
    gram, jac_mine = packed[:gram_rows], packed[gram_rows:]
    jac_other = swap(jac_mine, masks[0])
    solved = pl.pallas_call(
        solve_kernel,
        out_shape=jax.ShapeDtypeStruct((8, features), F32),
        scratch_shapes=[pltpu.VMEM((2, 8, 8, features), F32)],
        compiler_params=params,
        cost_estimate=pl.CostEstimate(
            flops=4 * 10**9, bytes_accessed=15 * 10**6, transcendentals=features
        ),
        name="solve",
    )(gram)
    value, flow, greeks, cot = pl.pallas_call(
        functools.partial(adjoint_kernel, assets, block),
        in_specs=[local] * 12,
        out_specs=[local] * 3 + [remote],
        out_shape=[short, short, jax.ShapeDtypeStruct((2, assets), F32), big],
        scratch_shapes=[
            pltpu.VMEM((12, assets, LANES), F32),
            pltpu.VMEM((2, 2, block // 16, LANES), F32),
            pltpu.VMEM((2, 3, block // LANES, LANES), F32),
            pltpu.VMEM((2, 2, assets, block), F32),
            pltpu.VMEM((assets, paths), F32),
            pltpu.VMEM((jac_rows, features), F32),
            pltpu.SemaphoreType.DMA((paths // (2 * block),)),
        ],
        compiler_params=params,
        name="adjoint",
    )(
        solved, jac_mine, jac_other, spot, vol, weights, cash.reshape(compact), taken.reshape(compact),
        value, pull, scaled, bounded,
    )
    return value.reshape(paths), cot, flow.reshape(paths), greeks


def solution(mesh):
    in_specs = (P(None, ("grp", "path")), P(), P(), P(), P(("grp", "path")), P(("grp", "path")))
    out_specs = (P(("grp", "path")), P(None, ("grp", "path")), P(("grp", "path")), P())
    return jax.shard_map(
        per_device, mesh=mesh, in_specs=in_specs, out_specs=out_specs, check_vma=False
    )
```

```python
import functools
import math

import jax
import jax.numpy as jnp
from jax import lax
from jax.experimental import pallas as pl
from jax.experimental.pallas import tpu as pltpu
from jax.sharding import PartitionSpec as P

root_time = math.sqrt(0.5)
notional = 20.0
soft_width = 0.02
LANES = 128
F32 = jnp.float32
BF16 = jnp.bfloat16
AXES = ("grp", "path")
CONTRACT_LAST = (((1,), (1,)), ((), ()))


def column(row, count):
    rows = lax.broadcasted_iota(jnp.int32, (count, count), 0)
    cols = lax.broadcasted_iota(jnp.int32, (count, count), 1)
    wide = jnp.broadcast_to(row, (count, count))
    picked = jnp.sum(jnp.where(rows == cols, wide, 0.0), axis=1, keepdims=True)
    return jnp.broadcast_to(picked, (count, LANES))


def split(x):
    hi = x.astype(BF16)
    lo = (x - hi.astype(F32)).astype(BF16)
    return hi, lo


def halves(rows):
    odd = lax.axis_index("path") & 1
    at = lambda index: pl.ds(pl.multiple_of(index * rows, 8), rows)
    return at(odd), at(1 - odd)


def sums_kernel(
    assets, width, spot, vol, weights, cash, taken, normals,
    scaled_out, bounded_out, value_out, pull_out, keep_out, give_out,
    small, flows, flags, draws, coef, part, target,
    scaled_all, bounded_all, value_all, pull_all, keep, give, slopes, rows_a, rows_b, acc, flow_acc, pull_acc, jac, sems, sent,
):
    features = 4 * assets
    paths = draws.shape[1]
    chunks = width // LANES
    blocks = paths // width
    copies = [
        pltpu.make_async_copy(spot, small.at[0:1, :], sems.at[0]),
        pltpu.make_async_copy(vol, small.at[1:2, :], sems.at[1]),
        pltpu.make_async_copy(weights, small.at[2:3, :], sems.at[2]),
        pltpu.make_async_copy(cash, flows, sems.at[3]),
        pltpu.make_async_copy(taken, flags, sems.at[4]),
    ]

    def pair(index):
        at = pl.ds(pl.multiple_of(index * (2 * width), 2 * width), 2 * width)
        return pltpu.make_async_copy(normals.at[:, at], draws.at[:, at], sems.at[5 + index])

    def leave(index):
        at = pl.ds(pl.multiple_of(index * (2 * width), 2 * width), 2 * width)
        line = pl.ds(pl.multiple_of(index * (2 * chunks), 2 * chunks), 2 * chunks)
        return [
            pltpu.make_async_copy(scaled_all.at[:, at], scaled_out.at[:, at], sent.at[0, index]),
            pltpu.make_async_copy(bounded_all.at[:, at], bounded_out.at[:, at], sent.at[1, index]),
            pltpu.make_async_copy(value_all.at[line, :], value_out.at[line, :], sent.at[2, index]),
            pltpu.make_async_copy(pull_all.at[line, :], pull_out.at[line, :], sent.at[3, index]),
        ]

    for copy in copies[:3]:
        copy.start()
    for index in range(blocks // 2):
        pair(index).start()
        if index == 0:
            for copy in copies[3:]:
                copy.start()
    acc[...] = jnp.zeros_like(acc)
    flow_acc[...] = jnp.zeros_like(flow_acc)
    pull_acc[...] = jnp.zeros_like(pull_acc)
    rows_b[...] = jnp.zeros_like(rows_b)
    target[...] = jnp.zeros_like(target)
    for copy in copies[:3]:
        copy.wait()
    spread = column(small[1:2, :] * root_time, assets)
    value = small[2:3, :] * small[0:1, :]
    total = jnp.sum(value, axis=1, keepdims=True)
    coef[0] = spread
    coef[1] = 0.5 * spread * spread
    coef[2] = 1.0 / spread
    coef[3] = column(value, assets) / jnp.broadcast_to(total, (assets, LANES))
    for copy in copies[3:]:
        copy.wait()

    last = lax.broadcasted_iota(jnp.int32, (assets, LANES), 0) == assets - 1
    aim, base, low = 10 * assets, 10 * assets + 16, 10 * assets + 16 + features

    def fill(block, rows, half):
        line = pl.ds(pl.multiple_of(block * chunks, chunks), chunks)
        flag = flags[line, :].astype(F32)
        flow = flows[line, :]
        rest = 1.0 - flag
        for c in range(half * chunks // 2, (half + 1) * chunks // 2):
            at = pl.ds(pl.multiple_of(block * width, width) + c * LANES, LANES)
            here = pl.ds(c * LANES, LANES)
            draw = draws[:, at]
            spread = coef[0]
            growth = jnp.exp(spread * draw - coef[1])
            weighted = growth * coef[3]
            part[8 * c : 8 * c + 8, :] = sum(weighted[8 * g : 8 * g + 8] for g in range(assets // 8))
            scaled = (growth - 1.0) * coef[2]
            bounded = jnp.where(last, 1.0, jnp.tanh(scaled))
            scaled_all[:, at] = scaled
            bounded_all[:, at] = bounded
            after = pltpu.roll(scaled, assets - 1, 0)
            before = pltpu.roll(scaled, 1, 0)
            kept = jnp.broadcast_to(rest[c : c + 1, :], (assets, LANES))
            for g, make in enumerate(
                [lambda: scaled, lambda: scaled * scaled - 1.0, lambda: scaled * after, lambda: bounded]
            ):
                wide = make()
                high = wide.astype(BF16)
                less = wide - high.astype(F32)
                if g == 3:
                    less = jnp.where(last, kept, less)
                rows[base + assets * g : base + assets * (g + 1), here] = high
                rows[low + assets * g : low + assets * (g + 1), here] = less.astype(BF16)
            slope = growth * (draw - spread) - scaled
            paid = jnp.broadcast_to(flow[c : c + 1, :], (assets, LANES))
            for g, make in enumerate(
                [
                    lambda: slope, lambda: slope * scaled, lambda: slope * after,
                    lambda: slope * (1.0 - bounded * bounded), lambda: slope * before,
                ]
            ):
                wide = make()
                high, less = split(wide)
                rows[assets * g : assets * (g + 1), here] = high
                rows[assets * (5 + g) : assets * (6 + g), here] = less
                flow_acc[assets * g : assets * (g + 1), :] += wide * paid
            slopes[:, here] = slope
        if half == 0:
            return
        basket = sum(part[pl.ds(i, chunks, stride=8), :] for i in range(8))
        x = (basket - 1.0) * (1.0 / soft_width)
        decay = jnp.exp(-jnp.abs(x))
        reward = (notional * soft_width) * (jnp.maximum(x, 0.0) + jnp.log1p(decay))
        inverse = 1.0 / (1.0 + decay)
        sigmoid = jnp.where(x >= 0.0, inverse, decay * inverse)
        pull = notional * flag * sigmoid
        value_all[line, :] = flag * reward
        pull_all[line, :] = pull
        flow_hi = flow.astype(BF16).astype(F32)
        pull_hi = pull.astype(BF16).astype(F32)
        pull_sum = 0.0
        for c in range(chunks):
            here = pl.ds(c * LANES, LANES)
            for index, row in enumerate([flow_hi, flow - flow_hi, rest, pull_hi, pull - pull_hi]):
                target[index : index + 1, here] = row[c : c + 1, :]
            pull_sum = pull_sum + slopes[:, here] * jnp.broadcast_to(pull[c : c + 1, :], (assets, LANES))
        pull_acc[...] += pull_sum
        rows[aim : aim + 16, :] = target[...].astype(BF16)

    cut = 16 * ((low // 16 + 1) // 2)

    def multiply(rows, part):
        at = slice(0, cut) if part == 0 else slice(cut, low)
        acc[at, :] += lax.dot_general(
            rows[at, :], rows[base:, :], CONTRACT_LAST, preferred_element_type=F32
        )

    def both(index, carry):
        pair(index).wait()
        for part in range(2):
            fill(2 * index, rows_a, part)
            multiply(rows_b, part)
        for part in range(2):
            fill(2 * index + 1, rows_b, part)
            multiply(rows_a, part)
        for copy in leave(index):
            copy.start()
        return carry

    lax.fori_loop(0, blocks // 2, both, 0)
    multiply(rows_b, 0)
    multiply(rows_b, 1)

    mid = features // 2
    high = acc[base:low, 0:features]
    cross = acc[base:low, features:]
    edge = lax.broadcasted_iota(jnp.int32, (features, features), 1) == features - 1
    half = 0.5 * high + jnp.where(edge, 0.0, cross)
    gram = half + half.T
    turned = pltpu.roll(gram[mid:, :], mid, 1)
    lanes = lax.broadcasted_iota(jnp.int32, (mid, features), 1)
    subs = lax.broadcasted_iota(jnp.int32, (mid, features), 0)
    packed = jnp.where(lanes >= subs, gram[0:mid, :], turned)
    keep[0:mid, :] = packed
    give[0:mid, :] = packed
    corner = jnp.sum(jnp.where(lanes == subs, turned, 0.0), axis=0, keepdims=True)
    aimed = acc[aim : aim + 8, 0:features] + jnp.where(edge[0:8], 0.0, acc[aim : aim + 8, features:])
    aims = jnp.concatenate(
        [
            aimed[0:1] + aimed[1:2], aimed[2:3], aimed[3:4] + aimed[4:5],
            jnp.zeros((5, features), F32),
        ],
        axis=0,
    )
    rank = lax.broadcasted_iota(jnp.int32, (8, features), 0)
    packed = jnp.where(rank == 3, jnp.broadcast_to(corner, (8, features)), aims)
    keep[mid : mid + 8, :] = packed
    give[mid : mid + 8, :] = packed
    five = 5 * assets
    edge = edge[0:1]
    leaned = acc[0:five, features:]
    full = acc[0:five, 0:features] + acc[five:aim, 0:features] + jnp.where(edge, 0.0, leaned)
    rest = jnp.sum(jnp.where(edge, leaned + acc[five:aim, features:], 0.0), axis=1, keepdims=True)
    flow = jnp.sum(flow_acc[...], axis=1, keepdims=True)
    pull = jnp.sum(pull_acc[...], axis=1, keepdims=True)
    jac[0:five, :] = full
    slots = lax.broadcasted_iota(jnp.int32, (five, features), 1)
    pull = jnp.concatenate([pull, jnp.zeros((4 * assets, 1), F32)], axis=0)
    sides = jnp.where(
        slots == 0, flow, jnp.where(slots == 1, rest, jnp.where(slots == 2, pull, 0.0))
    ).T
    jac[five : five + 8, :] = sides[0:8, 0:features]
    jac[five + 8 : five + 16, :] = jnp.concatenate(
        [sides[0:8, features:], jnp.zeros((8, features - assets), F32)], axis=1
    )
    mine, other = halves(jac.shape[0] // 2)
    keep[mid + 8 :, :] = jac[mine, :]
    give[mid + 8 :, :] = jac[other, :]
    last_copies = [
        pltpu.make_async_copy(give, give_out, sems.at[0]),
        pltpu.make_async_copy(keep, keep_out, sems.at[1]),
    ]
    for copy in last_copies:
        copy.start()
    for copy in last_copies:
        copy.wait()
    for index in range(blocks // 2):
        for copy in leave(index):
            copy.wait()


def lane(block, index):
    return jnp.broadcast_to(block[:, index : index + 1], block.shape)


def solve_kernel(packed, out, spread):
    features = packed.shape[1]
    blocks = features // 8
    mid = features // 2
    lanes = lax.broadcasted_iota(jnp.int32, (mid, features), 1)
    subs = lax.broadcasted_iota(jnp.int32, (mid, features), 0)
    upper = packed[0:mid, :]
    aims = packed[mid:, :]
    corner = jnp.broadcast_to(aims[3:4], (mid, features))
    lower = jnp.where(lanes < subs, upper, jnp.where(lanes == subs, 0.5 * corner, 0.0))
    half = jnp.concatenate(
        [
            jnp.where(lanes == subs, 0.5 * upper, jnp.where(lanes > subs, upper, 0.0)),
            pltpu.roll(lower, mid, 1),
        ],
        axis=0,
    )
    gram = half + half.T
    lanes = lax.broadcasted_iota(jnp.int32, (8, features), 1)
    subs = lax.broadcasted_iota(jnp.int32, (8, features), 0)
    mat = [gram[8 * v : 8 * v + 8, :] for v in range(blocks)] + [aims]
    for k in range(blocks):
        base = 8 * k
        head = mat[k]
        diag = {}
        for j in range(8):
            col = lane(head, base + j)
            spread[0, j] = col
            for i in range(j + 1):
                diag[i, j] = jnp.broadcast_to(spread[0, j, i : i + 1, :], (8, features))
        inside = (lanes >= base) & (lanes < base + 8)
        spread[1, 0] = jnp.where(inside, jnp.where(lanes == base + subs, -1.0, 0.0), head)
        work = [jnp.broadcast_to(spread[1, 0, i : i + 1, :], (8, features)) for i in range(8)]
        inverse, low = {}, {}
        for p in range(0, 8, 2):
            q = p + 1
            one, off, two = diag[p, p], diag[p, q], diag[q, q]
            inv = 1.0 / (one * two - off * off)
            inverse[p] = (two * inv, off * inv, one * inv)
            lift = {}
            for j in range(q + 1, 8):
                first, second = diag[p, j], diag[q, j]
                lift[j] = (two * first - off * second, one * second - off * first)
                low[p, j], low[q, j] = lift[j][0] * inv, lift[j][1] * inv
            for i in range(q + 1, 8):
                for j in range(i, 8):
                    drop = lift[i][0] * diag[p, j] + lift[i][1] * diag[q, j]
                    diag[i, j] = diag[i, j] - drop * inv
                work[i] = work[i] - (low[p, i] * work[p] + low[q, i] * work[q])
        for p in (6, 4, 2, 0):
            q = p + 1
            one, off, two = inverse[p]
            first = one * work[p] - off * work[q]
            second = two * work[q] - off * work[p]
            for j in reversed(range(q + 1, 8)):
                first = first - low[p, j] * work[j]
                second = second - low[q, j] * work[j]
            work[p], work[q] = first, second
        for v in range(k + 1, blocks + 1):
            new = jnp.where(inside, 0.0, mat[v])
            for c in reversed(range(8)):
                new = new - lane(mat[v], base + c) * work[c]
            mat[v] = new
    kept = jnp.broadcast_to(aims[2:3], (8, features))
    out[...] = jnp.where(subs == 3, kept, mat[blocks])


def adjoint_kernel(
    assets, width,
    solved, jac_mine, jac_other, spot, vol, weights, cash, taken,
    value_in, pull_in, scaled_in, bounded_in,
    value_out, flow_out, greeks_out, cot_out,
    coef, part, line, tangents, cot, jac, values, flows, greeks, sent,
):
    features = 4 * assets
    paths = scaled_in.shape[1]
    chunks = width // LANES
    turned = solved[...].T
    spread = column(vol[...] * root_time, assets)
    base = column(spot[...], assets)
    weight = column(weights[...], assets)
    total = jnp.sum(weights[...] * spot[...], axis=1, keepdims=True)
    offsets = []
    for which in range(2):
        parts = [
            jnp.broadcast_to(turned[assets * g : assets * (g + 1), which : which + 1], (assets, LANES))
            for g in range(4)
        ]
        for g in range(4):
            coef[5 * which + g] = parts[g]
        coef[5 * which + 4] = pltpu.roll(parts[2], 1, 0)
        offsets.append(jnp.sum(parts[1], axis=0, keepdims=True))
    coef[10] = 1.0 / (base * spread)
    coef[11] = weight / jnp.broadcast_to(total, (assets, LANES))

    def leave(index):
        at = pl.ds(pl.multiple_of(index * (2 * width), 2 * width), 2 * width)
        rows = pl.ds(pl.multiple_of(index * (2 * chunks), 2 * chunks), 2 * chunks)
        return [
            pltpu.make_async_copy(cot.at[:, at], cot_out.at[:, at], sent.at[0, index]),
            pltpu.make_async_copy(values.at[rows, :], value_out.at[rows, :], sent.at[1, index]),
            pltpu.make_async_copy(flows.at[rows, :], flow_out.at[rows, :], sent.at[2, index]),
        ]

    def block(index, slot):
        for c in range(chunks):
            at = pl.ds(pl.multiple_of(index * width, width) + c * LANES, LANES)
            here = pl.ds(c * LANES, LANES)
            scaled = scaled_in[:, at]
            bounded = bounded_in[:, at]
            after = pltpu.roll(scaled, assets - 1, 0)
            before = pltpu.roll(scaled, 1, 0)
            curve = 1.0 - bounded * bounded
            for which in range(2):
                k = 5 * which
                bend = coef[k + 1] * scaled
                inner = coef[k] + bend + coef[k + 2] * after
                terms = scaled * inner + coef[k + 3] * bounded
                part[slot, which, 8 * c : 8 * c + 8, :] = sum(
                    terms[8 * g : 8 * g + 8] for g in range(assets // 8)
                )
                tangents[slot, which, :, here] = (
                    inner + bend + coef[k + 4] * before + coef[k + 3] * curve
                )
        at = pl.ds(pl.multiple_of(index * chunks, chunks), chunks)
        fitted = [
            sum(part[slot, which, pl.ds(i, chunks, stride=8), :] for i in range(8)) - offsets[which]
            for which in range(2)
        ]
        rest = 1.0 - taken[at, :].astype(F32)
        values[at, :] = value_in[at, :] + rest * fitted[0]
        flows[at, :] = fitted[1]
        line[slot, 0] = cash[at, :] - fitted[0]
        line[slot, 1] = rest - fitted[1]
        line[slot, 2] = pull_in[at, :]
        for c in range(chunks):
            at = pl.ds(pl.multiple_of(index * width, width) + c * LANES, LANES)
            here = pl.ds(c * LANES, LANES)
            miss, gap, pull = (
                jnp.broadcast_to(line[slot, i, c : c + 1, :], (assets, LANES)) for i in range(3)
            )
            cot[:, at] = (
                miss * tangents[slot, 1, :, here] + gap * tangents[slot, 0, :, here]
            ) * coef[10] + pull * coef[11]

    def both(index, carry):
        block(2 * index, 0)
        block(2 * index + 1, 1)
        for copy in leave(index):
            copy.start()
        return carry

    mine, other = halves(jac_mine.shape[0])
    jac[mine, :] = jac_mine[...]
    jac[other, :] = jac_other[...]
    regression, multiplier = solved[0:1, :], solved[1:2, :]
    aims = features + assets
    against = lax.dot_general(
        solved[...], jac[0:aims, :], CONTRACT_LAST,
        precision=lax.Precision.HIGHEST, preferred_element_type=F32,
    )
    miss = jac[aims : aims + 1, :] - against[0:1, 0:features]
    gap = jac[aims + 1 : aims + 2, :] - against[1:2, 0:features]
    miss_side = jac[aims + 8 : aims + 9, 0:assets] - against[0:1, features:]
    gap_side = jac[aims + 9 : aims + 10, 0:assets] - against[1:2, features:]
    lanes = lax.broadcasted_iota(jnp.int32, (1, LANES), 1)
    double = jnp.where((lanes >= assets) & (lanes < 2 * assets), 2.0, 1.0)
    total = double * (multiplier * miss + regression * gap)
    total = total + pltpu.roll(total, 2 * assets, 1)
    total = total + pltpu.roll(total, assets, 1)

    def earlier(row):
        moved = pltpu.roll(row, features - 2 * assets + 1, 1)
        wrapped = pltpu.roll(row, features - 3 * assets + 1, 1)
        return jnp.where(lanes == 0, wrapped, moved)

    side = earlier(multiplier)[:, 0:assets] * miss_side + earlier(regression)[:, 0:assets] * gap_side
    vega = (total[:, 0:assets] + side) / vol[...]
    pulled_slope = jac[aims + 2 : aims + 3, 0:assets]
    pulled_scaled = solved[3:4, 0:assets]
    pulled = solved[3:4, features - 1 : features]
    value = weights[...] * spot[...]
    whole = jnp.sum(value, axis=1, keepdims=True)
    growth = pulled + vol[...] * root_time * pulled_scaled
    mean = jnp.sum(value * growth, axis=1, keepdims=True) / whole
    delta = weights[...] / whole * (growth - mean)
    vega = vega + value * root_time / whole * (pulled_slope + pulled_scaled)
    greeks[...] = jnp.concatenate([delta, vega], axis=0)
    whole_copy = pltpu.make_async_copy(greeks, greeks_out, sent.at[3, 0])
    whole_copy.start()
    lax.fori_loop(0, paths // (2 * width), both, 0)
    whole_copy.wait()
    for index in range(paths // (2 * width)):
        for copy in leave(index):
            copy.wait()


def swap(value, mask):
    count = math.prod(lax.axis_size(axis) for axis in AXES)
    return lax.ppermute(value, AXES, [(i, i ^ mask) for i in range(count)])


def gather_sum(value, masks):
    combos = [0]
    for mask in masks:
        combos = combos + [c ^ mask for c in combos]
    terms = [value] + [swap(value, c) for c in combos[1:]]
    while len(terms) > 1:
        terms = [a + b for a, b in zip(terms[::2], terms[1::2])]
    return terms[0]


def per_device(normals, spot, vol, weights, cash, taken):
    assets, paths = normals.shape
    features = 4 * assets
    path_total = paths * lax.axis_size("grp") * lax.axis_size("path")
    spot, vol, weights = (a.reshape(1, assets) for a in (spot, vol, weights))
    params = pltpu.CompilerParams(vmem_limit_bytes=16 * 1024 * 1024)
    big = jax.ShapeDtypeStruct((assets, paths), F32)
    jac_rows = features + assets + 16
    gram_rows = features // 2 + 8
    sent = jax.ShapeDtypeStruct((gram_rows + jac_rows // 2, features), F32)
    compact = (paths // LANES, LANES)
    block = 8 * LANES
    remote = pl.BlockSpec(memory_space=pltpu.HBM)
    local = pl.BlockSpec(memory_space=pltpu.VMEM)
    short = jax.ShapeDtypeStruct(compact, F32)
    wide = 16 * LANES
    rows = pltpu.VMEM((10 * assets + 16 + 2 * features, wide), BF16)
    scaled, bounded, value, pull, keep, give = pl.pallas_call(
        functools.partial(sums_kernel, assets, wide),
        in_specs=[remote] * 6,
        out_specs=[remote] * 6,
        out_shape=[
            big, big, short, short,
            sent, sent,
        ],
        scratch_shapes=[
            pltpu.VMEM((8, assets), F32),
            pltpu.VMEM(compact, F32),
            pltpu.VMEM(compact, jnp.int32),
            pltpu.VMEM((assets, paths), F32),
            pltpu.VMEM((4, assets, LANES), F32),
            pltpu.VMEM((wide // 16, LANES), F32),
            pltpu.VMEM((16, wide), F32),
            pltpu.VMEM((assets, paths), F32),
            pltpu.VMEM((assets, paths), F32),
            pltpu.VMEM(compact, F32),
            pltpu.VMEM(compact, F32),
            pltpu.VMEM(sent.shape, F32),
            pltpu.VMEM(sent.shape, F32),
            pltpu.VMEM((assets, wide), F32),
            rows, rows,
            pltpu.VMEM((10 * assets + 16 + features, 2 * features), F32),
            pltpu.VMEM((5 * assets, LANES), F32),
            pltpu.VMEM((assets, LANES), F32),
            pltpu.VMEM((jac_rows, features), F32),
            pltpu.SemaphoreType.DMA((5 + paths // (2 * wide),)),
            pltpu.SemaphoreType.DMA((4, paths // (2 * wide))),
        ],
        compiler_params=pltpu.CompilerParams(vmem_limit_bytes=60 * 1024 * 1024),
        name="sums",
    )(spot, vol, weights, cash.reshape(compact), taken.reshape(compact), normals)
    sizes = [lax.axis_size(axis) for axis in AXES]
    masks = [1 << bit for bit in range(math.prod(sizes).bit_length() - 1)]
    assert math.prod(sizes) == 1 << len(masks)
    scale = 1.0 / path_total
    packed = lax.optimization_barrier(keep * scale) + swap(give, masks[0]) * scale
    for group in [[masks[1], masks[-1]]] + [[mask] for mask in masks[2:-1]]:
        packed = gather_sum(packed, group)
    gram, jac_mine = packed[:gram_rows], packed[gram_rows:]
    jac_other = swap(jac_mine, masks[0])
    solved = pl.pallas_call(
        solve_kernel,
        out_shape=jax.ShapeDtypeStruct((8, features), F32),
        scratch_shapes=[pltpu.VMEM((2, 8, 8, features), F32)],
        compiler_params=params,
        cost_estimate=pl.CostEstimate(
            flops=4 * 10**9, bytes_accessed=15 * 10**6, transcendentals=features
        ),
        name="solve",
    )(gram)
    value, flow, greeks, cot = pl.pallas_call(
        functools.partial(adjoint_kernel, assets, block),
        in_specs=[local] * 12,
        out_specs=[remote] * 4,
        out_shape=[short, short, jax.ShapeDtypeStruct((2, assets), F32), big],
        scratch_shapes=[
            pltpu.VMEM((12, assets, LANES), F32),
            pltpu.VMEM((2, 2, block // 16, LANES), F32),
            pltpu.VMEM((2, 3, block // LANES, LANES), F32),
            pltpu.VMEM((2, 2, assets, block), F32),
            pltpu.VMEM((assets, paths), F32),
            pltpu.VMEM((jac_rows, features), F32),
            pltpu.VMEM(compact, F32),
            pltpu.VMEM(compact, F32),
            pltpu.VMEM((2, assets), F32),
            pltpu.SemaphoreType.DMA((4, paths // (2 * block))),
        ],
        compiler_params=params,
        name="adjoint",
    )(
        solved, jac_mine, jac_other, spot, vol, weights, cash.reshape(compact), taken.reshape(compact),
        value, pull, scaled, bounded,
    )
    return value.reshape(paths), cot, flow.reshape(paths), greeks


def solution(mesh):
    in_specs = (P(None, ("grp", "path")), P(), P(), P(), P(("grp", "path")), P(("grp", "path")))
    out_specs = (P(("grp", "path")), P(None, ("grp", "path")), P(("grp", "path")), P())
    return jax.shard_map(
        per_device, mesh=mesh, in_specs=in_specs, out_specs=out_specs, check_vma=False
    )
```

```python
import functools
import math

import jax
import jax.numpy as jnp
from jax import lax
from jax.experimental import pallas as pl
from jax.experimental.pallas import tpu as pltpu
from jax.sharding import PartitionSpec as P

root_time = math.sqrt(0.5)
notional = 20.0
soft_width = 0.02
LANES = 128
F32 = jnp.float32
BF16 = jnp.bfloat16
AXES = ("grp", "path")
CONTRACT_LAST = (((1,), (1,)), ((), ()))


def column(row, count):
    rows = lax.broadcasted_iota(jnp.int32, (count, count), 0)
    cols = lax.broadcasted_iota(jnp.int32, (count, count), 1)
    wide = jnp.broadcast_to(row, (count, count))
    picked = jnp.sum(jnp.where(rows == cols, wide, 0.0), axis=1, keepdims=True)
    return jnp.broadcast_to(picked, (count, LANES))


def split(x):
    hi = x.astype(BF16)
    lo = (x - hi.astype(F32)).astype(BF16)
    return hi, lo


def halves(rows):
    odd = lax.axis_index("path") & 1
    at = lambda index: pl.ds(pl.multiple_of(index * rows, 8), rows)
    return at(odd), at(1 - odd)


def sums_kernel(
    assets, width, spot, vol, weights, cash, taken, normals,
    scaled_out, bounded_out, value_out, pull_out, keep_out, give_out,
    small, flows, flags, draws, coef, part, target,
    scaled_all, bounded_all, value_all, pull_all, keep, give, slopes, rows_a, rows_b, acc, flow_acc, pull_acc, jac, sems, sent,
):
    features = 4 * assets
    paths = draws.shape[1]
    chunks = width // LANES
    blocks = paths // width
    copies = [
        pltpu.make_async_copy(spot, small.at[0:1, :], sems.at[0]),
        pltpu.make_async_copy(vol, small.at[1:2, :], sems.at[1]),
        pltpu.make_async_copy(weights, small.at[2:3, :], sems.at[2]),
        pltpu.make_async_copy(cash, flows, sems.at[3]),
        pltpu.make_async_copy(taken, flags, sems.at[4]),
    ]

    def pair(index):
        at = pl.ds(pl.multiple_of(index * (2 * width), 2 * width), 2 * width)
        return pltpu.make_async_copy(normals.at[:, at], draws.at[:, at], sems.at[5 + index])

    def leave(index):
        at = pl.ds(pl.multiple_of(index * (2 * width), 2 * width), 2 * width)
        line = pl.ds(pl.multiple_of(index * (2 * chunks), 2 * chunks), 2 * chunks)
        return [
            pltpu.make_async_copy(scaled_all.at[:, at], scaled_out.at[:, at], sent.at[0, index]),
            pltpu.make_async_copy(bounded_all.at[:, at], bounded_out.at[:, at], sent.at[1, index]),
            pltpu.make_async_copy(value_all.at[line, :], value_out.at[line, :], sent.at[2, index]),
            pltpu.make_async_copy(pull_all.at[line, :], pull_out.at[line, :], sent.at[3, index]),
        ]

    for copy in copies[:3]:
        copy.start()
    for index in range(blocks // 2):
        pair(index).start()
        if index == 0:
            for copy in copies[3:]:
                copy.start()
    acc[...] = jnp.zeros_like(acc)
    flow_acc[...] = jnp.zeros_like(flow_acc)
    pull_acc[...] = jnp.zeros_like(pull_acc)
    rows_b[...] = jnp.zeros_like(rows_b)
    target[...] = jnp.zeros_like(target)
    for copy in copies[:3]:
        copy.wait()
    spread = column(small[1:2, :] * root_time, assets)
    value = small[2:3, :] * small[0:1, :]
    total = jnp.sum(value, axis=1, keepdims=True)
    coef[0] = spread
    coef[1] = 0.5 * spread * spread
    coef[2] = 1.0 / spread
    coef[3] = column(value, assets) / jnp.broadcast_to(total, (assets, LANES))
    for copy in copies[3:]:
        copy.wait()

    last = lax.broadcasted_iota(jnp.int32, (assets, LANES), 0) == assets - 1
    aim, base, low = 10 * assets, 10 * assets + 16, 10 * assets + 16 + features

    def fill(block, rows, half):
        line = pl.ds(pl.multiple_of(block * chunks, chunks), chunks)
        flag = flags[line, :].astype(F32)
        flow = flows[line, :]
        rest = 1.0 - flag
        for c in range(half * chunks // 2, (half + 1) * chunks // 2):
            at = pl.ds(pl.multiple_of(block * width, width) + c * LANES, LANES)
            here = pl.ds(c * LANES, LANES)
            draw = draws[:, at]
            spread = coef[0]
            growth = jnp.exp(spread * draw - coef[1])
            weighted = growth * coef[3]
            part[8 * c : 8 * c + 8, :] = sum(weighted[8 * g : 8 * g + 8] for g in range(assets // 8))
            scaled = (growth - 1.0) * coef[2]
            bounded = jnp.where(last, 1.0, jnp.tanh(scaled))
            scaled_all[:, at] = scaled
            bounded_all[:, at] = bounded
            after = pltpu.roll(scaled, assets - 1, 0)
            before = pltpu.roll(scaled, 1, 0)
            kept = jnp.broadcast_to(rest[c : c + 1, :], (assets, LANES))
            for g, make in enumerate(
                [lambda: scaled, lambda: scaled * scaled - 1.0, lambda: scaled * after, lambda: bounded]
            ):
                wide = make()
                high = wide.astype(BF16)
                less = wide - high.astype(F32)
                if g == 3:
                    less = jnp.where(last, kept, less)
                rows[base + assets * g : base + assets * (g + 1), here] = high
                rows[low + assets * g : low + assets * (g + 1), here] = less.astype(BF16)
            slope = growth * (draw - spread) - scaled
            paid = jnp.broadcast_to(flow[c : c + 1, :], (assets, LANES))
            for g, make in enumerate(
                [
                    lambda: slope, lambda: slope * scaled, lambda: slope * after,
                    lambda: slope * (1.0 - bounded * bounded), lambda: slope * before,
                ]
            ):
                wide = make()
                high, less = split(wide)
                rows[assets * g : assets * (g + 1), here] = high
                rows[assets * (5 + g) : assets * (6 + g), here] = less
                flow_acc[assets * g : assets * (g + 1), :] += wide * paid
            slopes[:, here] = slope
        if half == 0:
            return
        basket = sum(part[pl.ds(i, chunks, stride=8), :] for i in range(8))
        x = (basket - 1.0) * (1.0 / soft_width)
        decay = jnp.exp(-jnp.abs(x))
        reward = (notional * soft_width) * (jnp.maximum(x, 0.0) + jnp.log1p(decay))
        inverse = 1.0 / (1.0 + decay)
        sigmoid = jnp.where(x >= 0.0, inverse, decay * inverse)
        pull = notional * flag * sigmoid
        value_all[line, :] = flag * reward
        pull_all[line, :] = pull
        flow_hi = flow.astype(BF16).astype(F32)
        pull_hi = pull.astype(BF16).astype(F32)
        pull_sum = 0.0
        for c in range(chunks):
            here = pl.ds(c * LANES, LANES)
            for index, row in enumerate([flow_hi, flow - flow_hi, rest, pull_hi, pull - pull_hi]):
                target[index : index + 1, here] = row[c : c + 1, :]
            pull_sum = pull_sum + slopes[:, here] * jnp.broadcast_to(pull[c : c + 1, :], (assets, LANES))
        pull_acc[...] += pull_sum
        rows[aim : aim + 16, :] = target[...].astype(BF16)

    cut = 2 * features

    def multiply(rows, part):
        at = slice(0, cut) if part == 0 else slice(cut, low)
        acc[at, :] += lax.dot_general(
            rows[at, :], rows[base:, :], CONTRACT_LAST, preferred_element_type=F32
        )

    def both(index, carry):
        pair(index).wait()
        for part in range(2):
            fill(2 * index, rows_a, part)
            multiply(rows_b, part)
        for part in range(2):
            fill(2 * index + 1, rows_b, part)
            multiply(rows_a, part)
        for copy in leave(index):
            copy.start()
        return carry

    lax.fori_loop(0, blocks // 2, both, 0)
    multiply(rows_b, 0)
    multiply(rows_b, 1)

    mid = features // 2
    high = acc[base:low, 0:features]
    cross = acc[base:low, features:]
    edge = lax.broadcasted_iota(jnp.int32, (features, features), 1) == features - 1
    half = 0.5 * high + jnp.where(edge, 0.0, cross)
    gram = half + half.T
    turned = pltpu.roll(gram[mid:, :], mid, 1)
    lanes = lax.broadcasted_iota(jnp.int32, (mid, features), 1)
    subs = lax.broadcasted_iota(jnp.int32, (mid, features), 0)
    packed = jnp.where(lanes >= subs, gram[0:mid, :], turned)
    keep[0:mid, :] = packed
    give[0:mid, :] = packed
    corner = jnp.sum(jnp.where(lanes == subs, turned, 0.0), axis=0, keepdims=True)
    aimed = acc[aim : aim + 8, 0:features] + jnp.where(edge[0:8], 0.0, acc[aim : aim + 8, features:])
    aims = jnp.concatenate(
        [
            aimed[0:1] + aimed[1:2], aimed[2:3], aimed[3:4] + aimed[4:5],
            jnp.zeros((5, features), F32),
        ],
        axis=0,
    )
    rank = lax.broadcasted_iota(jnp.int32, (8, features), 0)
    packed = jnp.where(rank == 3, jnp.broadcast_to(corner, (8, features)), aims)
    keep[mid : mid + 8, :] = packed
    give[mid : mid + 8, :] = packed
    five = 5 * assets
    edge = edge[0:1]
    leaned = acc[0:five, features:]
    full = acc[0:five, 0:features] + acc[five:aim, 0:features] + jnp.where(edge, 0.0, leaned)
    rest = jnp.sum(jnp.where(edge, leaned + acc[five:aim, features:], 0.0), axis=1, keepdims=True)
    flow = jnp.sum(flow_acc[...], axis=1, keepdims=True)
    pull = jnp.sum(pull_acc[...], axis=1, keepdims=True)
    jac[0:five, :] = full
    slots = lax.broadcasted_iota(jnp.int32, (five, features), 1)
    pull = jnp.concatenate([pull, jnp.zeros((4 * assets, 1), F32)], axis=0)
    sides = jnp.where(
        slots == 0, flow, jnp.where(slots == 1, rest, jnp.where(slots == 2, pull, 0.0))
    ).T
    jac[five : five + 8, :] = sides[0:8, 0:features]
    jac[five + 8 : five + 16, :] = jnp.concatenate(
        [sides[0:8, features:], jnp.zeros((8, features - assets), F32)], axis=1
    )
    mine, other = halves(jac.shape[0] // 2)
    keep[mid + 8 :, :] = jac[mine, :]
    give[mid + 8 :, :] = jac[other, :]
    last_copies = [
        pltpu.make_async_copy(give, give_out, sems.at[0]),
        pltpu.make_async_copy(keep, keep_out, sems.at[1]),
    ]
    for copy in last_copies:
        copy.start()
    for copy in last_copies:
        copy.wait()
    for index in range(blocks // 2):
        for copy in leave(index):
            copy.wait()


def lane(block, index):
    return jnp.broadcast_to(block[:, index : index + 1], block.shape)


def solve_kernel(packed, out, spread):
    features = packed.shape[1]
    blocks = features // 8
    mid = features // 2
    lanes = lax.broadcasted_iota(jnp.int32, (mid, features), 1)
    subs = lax.broadcasted_iota(jnp.int32, (mid, features), 0)
    upper = packed[0:mid, :]
    aims = packed[mid:, :]
    corner = jnp.broadcast_to(aims[3:4], (mid, features))
    lower = jnp.where(lanes < subs, upper, jnp.where(lanes == subs, 0.5 * corner, 0.0))
    half = jnp.concatenate(
        [
            jnp.where(lanes == subs, 0.5 * upper, jnp.where(lanes > subs, upper, 0.0)),
            pltpu.roll(lower, mid, 1),
        ],
        axis=0,
    )
    gram = half + half.T
    lanes = lax.broadcasted_iota(jnp.int32, (8, features), 1)
    subs = lax.broadcasted_iota(jnp.int32, (8, features), 0)
    mat = [gram[8 * v : 8 * v + 8, :] for v in range(blocks)] + [aims]
    for k in range(blocks):
        base = 8 * k
        head = mat[k]
        diag = {}
        for j in range(8):
            col = lane(head, base + j)
            spread[0, j] = col
            for i in range(j + 1):
                diag[i, j] = jnp.broadcast_to(spread[0, j, i : i + 1, :], (8, features))
        inside = (lanes >= base) & (lanes < base + 8)
        spread[1, 0] = jnp.where(inside, jnp.where(lanes == base + subs, -1.0, 0.0), head)
        work = [jnp.broadcast_to(spread[1, 0, i : i + 1, :], (8, features)) for i in range(8)]
        inverse, low = {}, {}
        for p in range(0, 8, 2):
            q = p + 1
            one, off, two = diag[p, p], diag[p, q], diag[q, q]
            inv = 1.0 / (one * two - off * off)
            inverse[p] = (two * inv, off * inv, one * inv)
            lift = {}
            for j in range(q + 1, 8):
                first, second = diag[p, j], diag[q, j]
                lift[j] = (two * first - off * second, one * second - off * first)
                low[p, j], low[q, j] = lift[j][0] * inv, lift[j][1] * inv
            for i in range(q + 1, 8):
                for j in range(i, 8):
                    drop = lift[i][0] * diag[p, j] + lift[i][1] * diag[q, j]
                    diag[i, j] = diag[i, j] - drop * inv
                work[i] = work[i] - (low[p, i] * work[p] + low[q, i] * work[q])
        for p in (6, 4, 2, 0):
            q = p + 1
            one, off, two = inverse[p]
            first = one * work[p] - off * work[q]
            second = two * work[q] - off * work[p]
            for j in reversed(range(q + 1, 8)):
                first = first - low[p, j] * work[j]
                second = second - low[q, j] * work[j]
            work[p], work[q] = first, second
        for v in range(k + 1, blocks + 1):
            new = jnp.where(inside, 0.0, mat[v])
            for c in reversed(range(8)):
                new = new - lane(mat[v], base + c) * work[c]
            mat[v] = new
    kept = jnp.broadcast_to(aims[2:3], (8, features))
    out[...] = jnp.where(subs == 3, kept, mat[blocks])


def adjoint_kernel(
    assets, width,
    solved, jac_mine, jac_other, spot, vol, weights, cash, taken,
    value_in, pull_in, scaled_in, bounded_in,
    value_out, flow_out, greeks_out, cot_out,
    coef, part, line, tangents, cot, jac, values, flows, greeks, sent,
):
    features = 4 * assets
    paths = scaled_in.shape[1]
    chunks = width // LANES
    turned = solved[...].T
    spread = column(vol[...] * root_time, assets)
    base = column(spot[...], assets)
    weight = column(weights[...], assets)
    total = jnp.sum(weights[...] * spot[...], axis=1, keepdims=True)
    offsets = []
    for which in range(2):
        parts = [
            jnp.broadcast_to(turned[assets * g : assets * (g + 1), which : which + 1], (assets, LANES))
            for g in range(4)
        ]
        for g in range(4):
            coef[5 * which + g] = parts[g]
        coef[5 * which + 4] = pltpu.roll(parts[2], 1, 0)
        offsets.append(jnp.sum(parts[1], axis=0, keepdims=True))
    coef[10] = 1.0 / (base * spread)
    coef[11] = weight / jnp.broadcast_to(total, (assets, LANES))

    def leave(index):
        at = pl.ds(pl.multiple_of(index * (2 * width), 2 * width), 2 * width)
        rows = pl.ds(pl.multiple_of(index * (2 * chunks), 2 * chunks), 2 * chunks)
        return [
            pltpu.make_async_copy(cot.at[:, at], cot_out.at[:, at], sent.at[0, index]),
            pltpu.make_async_copy(values.at[rows, :], value_out.at[rows, :], sent.at[1, index]),
            pltpu.make_async_copy(flows.at[rows, :], flow_out.at[rows, :], sent.at[2, index]),
        ]

    def block(index, slot):
        for c in range(chunks):
            at = pl.ds(pl.multiple_of(index * width, width) + c * LANES, LANES)
            here = pl.ds(c * LANES, LANES)
            scaled = scaled_in[:, at]
            bounded = bounded_in[:, at]
            after = pltpu.roll(scaled, assets - 1, 0)
            before = pltpu.roll(scaled, 1, 0)
            curve = 1.0 - bounded * bounded
            for which in range(2):
                k = 5 * which
                bend = coef[k + 1] * scaled
                inner = coef[k] + bend + coef[k + 2] * after
                terms = scaled * inner + coef[k + 3] * bounded
                part[slot, which, 8 * c : 8 * c + 8, :] = sum(
                    terms[8 * g : 8 * g + 8] for g in range(assets // 8)
                )
                tangents[slot, which, :, here] = (
                    inner + bend + coef[k + 4] * before + coef[k + 3] * curve
                )
        at = pl.ds(pl.multiple_of(index * chunks, chunks), chunks)
        fitted = [
            sum(part[slot, which, pl.ds(i, chunks, stride=8), :] for i in range(8)) - offsets[which]
            for which in range(2)
        ]
        rest = 1.0 - taken[at, :].astype(F32)
        values[at, :] = value_in[at, :] + rest * fitted[0]
        flows[at, :] = fitted[1]
        line[slot, 0] = cash[at, :] - fitted[0]
        line[slot, 1] = rest - fitted[1]
        line[slot, 2] = pull_in[at, :]
        for c in range(chunks):
            at = pl.ds(pl.multiple_of(index * width, width) + c * LANES, LANES)
            here = pl.ds(c * LANES, LANES)
            miss, gap, pull = (
                jnp.broadcast_to(line[slot, i, c : c + 1, :], (assets, LANES)) for i in range(3)
            )
            cot[:, at] = (
                miss * tangents[slot, 1, :, here] + gap * tangents[slot, 0, :, here]
            ) * coef[10] + pull * coef[11]

    def both(index, carry):
        block(2 * index, 0)
        block(2 * index + 1, 1)
        for copy in leave(index):
            copy.start()
        return carry

    mine, other = halves(jac_mine.shape[0])
    jac[mine, :] = jac_mine[...]
    jac[other, :] = jac_other[...]
    regression, multiplier = solved[0:1, :], solved[1:2, :]
    aims = features + assets
    against = lax.dot_general(
        solved[...], jac[0:aims, :], CONTRACT_LAST,
        precision=lax.Precision.HIGHEST, preferred_element_type=F32,
    )
    miss = jac[aims : aims + 1, :] - against[0:1, 0:features]
    gap = jac[aims + 1 : aims + 2, :] - against[1:2, 0:features]
    miss_side = jac[aims + 8 : aims + 9, 0:assets] - against[0:1, features:]
    gap_side = jac[aims + 9 : aims + 10, 0:assets] - against[1:2, features:]
    lanes = lax.broadcasted_iota(jnp.int32, (1, LANES), 1)
    double = jnp.where((lanes >= assets) & (lanes < 2 * assets), 2.0, 1.0)
    total = double * (multiplier * miss + regression * gap)
    total = total + pltpu.roll(total, 2 * assets, 1)
    total = total + pltpu.roll(total, assets, 1)

    def earlier(row):
        moved = pltpu.roll(row, features - 2 * assets + 1, 1)
        wrapped = pltpu.roll(row, features - 3 * assets + 1, 1)
        return jnp.where(lanes == 0, wrapped, moved)

    side = earlier(multiplier)[:, 0:assets] * miss_side + earlier(regression)[:, 0:assets] * gap_side
    vega = (total[:, 0:assets] + side) / vol[...]
    pulled_slope = jac[aims + 2 : aims + 3, 0:assets]
    pulled_scaled = solved[3:4, 0:assets]
    pulled = solved[3:4, features - 1 : features]
    value = weights[...] * spot[...]
    whole = jnp.sum(value, axis=1, keepdims=True)
    growth = pulled + vol[...] * root_time * pulled_scaled
    mean = jnp.sum(value * growth, axis=1, keepdims=True) / whole
    delta = weights[...] / whole * (growth - mean)
    vega = vega + value * root_time / whole * (pulled_slope + pulled_scaled)
    greeks[...] = jnp.concatenate([delta, vega], axis=0)
    whole_copy = pltpu.make_async_copy(greeks, greeks_out, sent.at[3, 0])
    whole_copy.start()
    lax.fori_loop(0, paths // (2 * width), both, 0)
    whole_copy.wait()
    for index in range(paths // (2 * width)):
        for copy in leave(index):
            copy.wait()


def swap(value, mask):
    count = math.prod(lax.axis_size(axis) for axis in AXES)
    return lax.ppermute(value, AXES, [(i, i ^ mask) for i in range(count)])


def gather_sum(value, masks):
    combos = [0]
    for mask in masks:
        combos = combos + [c ^ mask for c in combos]
    terms = [value] + [swap(value, c) for c in combos[1:]]
    while len(terms) > 1:
        terms = [a + b for a, b in zip(terms[::2], terms[1::2])]
    return terms[0]


def per_device(normals, spot, vol, weights, cash, taken):
    assets, paths = normals.shape
    features = 4 * assets
    path_total = paths * lax.axis_size("grp") * lax.axis_size("path")
    spot, vol, weights = (a.reshape(1, assets) for a in (spot, vol, weights))
    params = pltpu.CompilerParams(vmem_limit_bytes=16 * 1024 * 1024)
    big = jax.ShapeDtypeStruct((assets, paths), F32)
    jac_rows = features + assets + 16
    gram_rows = features // 2 + 8
    sent = jax.ShapeDtypeStruct((gram_rows + jac_rows // 2, features), F32)
    compact = (paths // LANES, LANES)
    block = 8 * LANES
    remote = pl.BlockSpec(memory_space=pltpu.HBM)
    local = pl.BlockSpec(memory_space=pltpu.VMEM)
    short = jax.ShapeDtypeStruct(compact, F32)
    wide = 16 * LANES
    rows = pltpu.VMEM((10 * assets + 16 + 2 * features, wide), BF16)
    scaled, bounded, value, pull, keep, give = pl.pallas_call(
        functools.partial(sums_kernel, assets, wide),
        in_specs=[remote] * 6,
        out_specs=[remote] * 6,
        out_shape=[
            big, big, short, short,
            sent, sent,
        ],
        scratch_shapes=[
            pltpu.VMEM((8, assets), F32),
            pltpu.VMEM(compact, F32),
            pltpu.VMEM(compact, jnp.int32),
            pltpu.VMEM((assets, paths), F32),
            pltpu.VMEM((4, assets, LANES), F32),
            pltpu.VMEM((wide // 16, LANES), F32),
            pltpu.VMEM((16, wide), F32),
            pltpu.VMEM((assets, paths), F32),
            pltpu.VMEM((assets, paths), F32),
            pltpu.VMEM(compact, F32),
            pltpu.VMEM(compact, F32),
            pltpu.VMEM(sent.shape, F32),
            pltpu.VMEM(sent.shape, F32),
            pltpu.VMEM((assets, wide), F32),
            rows, rows,
            pltpu.VMEM((10 * assets + 16 + features, 2 * features), F32),
            pltpu.VMEM((5 * assets, LANES), F32),
            pltpu.VMEM((assets, LANES), F32),
            pltpu.VMEM((jac_rows, features), F32),
            pltpu.SemaphoreType.DMA((5 + paths // (2 * wide),)),
            pltpu.SemaphoreType.DMA((4, paths // (2 * wide))),
        ],
        compiler_params=pltpu.CompilerParams(vmem_limit_bytes=60 * 1024 * 1024),
        name="sums",
    )(spot, vol, weights, cash.reshape(compact), taken.reshape(compact), normals)
    sizes = [lax.axis_size(axis) for axis in AXES]
    masks = [1 << bit for bit in range(math.prod(sizes).bit_length() - 1)]
    assert math.prod(sizes) == 1 << len(masks)
    scale = 1.0 / path_total
    packed = lax.optimization_barrier(keep * scale) + swap(give, masks[0]) * scale
    for group in [[masks[1], masks[-1]]] + [[mask] for mask in masks[2:-1]]:
        packed = gather_sum(packed, group)
    gram, jac_mine = packed[:gram_rows], packed[gram_rows:]
    jac_other = swap(jac_mine, masks[0])
    solved = pl.pallas_call(
        solve_kernel,
        out_shape=jax.ShapeDtypeStruct((8, features), F32),
        scratch_shapes=[pltpu.VMEM((2, 8, 8, features), F32)],
        compiler_params=params,
        cost_estimate=pl.CostEstimate(
            flops=4 * 10**9, bytes_accessed=15 * 10**6, transcendentals=features
        ),
        name="solve",
    )(gram)
    value, flow, greeks, cot = pl.pallas_call(
        functools.partial(adjoint_kernel, assets, wide),
        in_specs=[local] * 12,
        out_specs=[remote] * 4,
        out_shape=[short, short, jax.ShapeDtypeStruct((2, assets), F32), big],
        scratch_shapes=[
            pltpu.VMEM((12, assets, LANES), F32),
            pltpu.VMEM((2, 2, wide // 16, LANES), F32),
            pltpu.VMEM((2, 3, wide // LANES, LANES), F32),
            pltpu.VMEM((2, 2, assets, wide), F32),
            pltpu.VMEM((assets, paths), F32),
            pltpu.VMEM((jac_rows, features), F32),
            pltpu.VMEM(compact, F32),
            pltpu.VMEM(compact, F32),
            pltpu.VMEM((2, assets), F32),
            pltpu.SemaphoreType.DMA((4, paths // (2 * wide))),
        ],
        compiler_params=params,
        name="adjoint",
    )(
        solved, jac_mine, jac_other, spot, vol, weights, cash.reshape(compact), taken.reshape(compact),
        value, pull, scaled, bounded,
    )
    return value.reshape(paths), cot, flow.reshape(paths), greeks


def solution(mesh):
    in_specs = (P(None, ("grp", "path")), P(), P(), P(), P(("grp", "path")), P(("grp", "path")))
    out_specs = (P(("grp", "path")), P(None, ("grp", "path")), P(("grp", "path")), P())
    return jax.shard_map(
        per_device, mesh=mesh, in_specs=in_specs, out_specs=out_specs, check_vma=False
    )
```

```python
import functools
import math

import jax
import jax.numpy as jnp
from jax import lax
from jax.experimental import pallas as pl
from jax.experimental.pallas import tpu as pltpu
from jax.sharding import PartitionSpec as P

root_time = math.sqrt(0.5)
notional = 20.0
soft_width = 0.02
LANES = 128
F32 = jnp.float32
BF16 = jnp.bfloat16
AXES = ("grp", "path")
CONTRACT_LAST = (((1,), (1,)), ((), ()))


def column(row, count):
    rows = lax.broadcasted_iota(jnp.int32, (count, count), 0)
    cols = lax.broadcasted_iota(jnp.int32, (count, count), 1)
    wide = jnp.broadcast_to(row, (count, count))
    picked = jnp.sum(jnp.where(rows == cols, wide, 0.0), axis=1, keepdims=True)
    return jnp.broadcast_to(picked, (count, LANES))


def split(x):
    hi = x.astype(BF16)
    lo = (x - hi.astype(F32)).astype(BF16)
    return hi, lo


def halves(rows):
    odd = lax.axis_index("path") & 1
    at = lambda index: pl.ds(pl.multiple_of(index * rows, 8), rows)
    return at(odd), at(1 - odd)


def sums_kernel(
    assets, width, spot, vol, weights, cash, taken, normals,
    scaled_out, bounded_out, value_out, pull_out, keep_out, give_out,
    small, flows, flags, draws, coef, part, target,
    scaled_all, bounded_all, value_all, pull_all, keep, give, slopes, rows_a, rows_b, acc, flow_acc, pull_acc, jac, sems, sent,
):
    features = 4 * assets
    paths = draws.shape[1]
    chunks = width // LANES
    blocks = paths // width
    copies = [
        pltpu.make_async_copy(spot, small.at[0:1, :], sems.at[0]),
        pltpu.make_async_copy(vol, small.at[1:2, :], sems.at[1]),
        pltpu.make_async_copy(weights, small.at[2:3, :], sems.at[2]),
        pltpu.make_async_copy(cash, flows, sems.at[3]),
        pltpu.make_async_copy(taken, flags, sems.at[4]),
    ]

    def pair(index):
        at = pl.ds(pl.multiple_of(index * (2 * width), 2 * width), 2 * width)
        return pltpu.make_async_copy(normals.at[:, at], draws.at[:, at], sems.at[5 + index])

    def leave(index):
        at = pl.ds(pl.multiple_of(index * (2 * width), 2 * width), 2 * width)
        line = pl.ds(pl.multiple_of(index * (2 * chunks), 2 * chunks), 2 * chunks)
        return [
            pltpu.make_async_copy(scaled_all.at[:, at], scaled_out.at[:, at], sent.at[0, index]),
            pltpu.make_async_copy(bounded_all.at[:, at], bounded_out.at[:, at], sent.at[1, index]),
            pltpu.make_async_copy(value_all.at[line, :], value_out.at[line, :], sent.at[2, index]),
            pltpu.make_async_copy(pull_all.at[line, :], pull_out.at[line, :], sent.at[3, index]),
        ]

    for copy in copies[:3]:
        copy.start()
    for index in range(blocks // 2):
        pair(index).start()
        if index == 0:
            for copy in copies[3:]:
                copy.start()
    acc[...] = jnp.zeros_like(acc)
    flow_acc[...] = jnp.zeros_like(flow_acc)
    pull_acc[...] = jnp.zeros_like(pull_acc)
    rows_b[...] = jnp.zeros_like(rows_b)
    target[...] = jnp.zeros_like(target)
    for copy in copies[:3]:
        copy.wait()
    spread = column(small[1:2, :] * root_time, assets)
    value = small[2:3, :] * small[0:1, :]
    total = jnp.sum(value, axis=1, keepdims=True)
    coef[0] = spread
    coef[1] = 0.5 * spread * spread
    coef[2] = 1.0 / spread
    coef[3] = column(value, assets) / jnp.broadcast_to(total, (assets, LANES))
    for copy in copies[3:]:
        copy.wait()

    last = lax.broadcasted_iota(jnp.int32, (assets, LANES), 0) == assets - 1
    aim, base, low = 10 * assets, 10 * assets + 16, 10 * assets + 16 + features

    def fill(block, rows, half):
        line = pl.ds(pl.multiple_of(block * chunks, chunks), chunks)
        flag = flags[line, :].astype(F32)
        flow = flows[line, :]
        rest = 1.0 - flag
        for c in range(half * chunks // 2, (half + 1) * chunks // 2):
            at = pl.ds(pl.multiple_of(block * width, width) + c * LANES, LANES)
            here = pl.ds(c * LANES, LANES)
            draw = draws[:, at]
            spread = coef[0]
            growth = jnp.exp(spread * draw - coef[1])
            weighted = growth * coef[3]
            part[8 * c : 8 * c + 8, :] = sum(weighted[8 * g : 8 * g + 8] for g in range(assets // 8))
            scaled = (growth - 1.0) * coef[2]
            bounded = jnp.where(last, 1.0, jnp.tanh(scaled))
            scaled_all[:, at] = scaled
            bounded_all[:, at] = bounded
            after = pltpu.roll(scaled, assets - 1, 0)
            before = pltpu.roll(scaled, 1, 0)
            kept = jnp.broadcast_to(rest[c : c + 1, :], (assets, LANES))
            for g, make in enumerate(
                [lambda: scaled, lambda: scaled * scaled - 1.0, lambda: scaled * after, lambda: bounded]
            ):
                wide = make()
                high = wide.astype(BF16)
                less = wide - high.astype(F32)
                if g == 3:
                    less = jnp.where(last, kept, less)
                rows[base + assets * g : base + assets * (g + 1), here] = high
                rows[low + assets * g : low + assets * (g + 1), here] = less.astype(BF16)
            slope = growth * (draw - spread) - scaled
            paid = jnp.broadcast_to(flow[c : c + 1, :], (assets, LANES))
            for g, make in enumerate(
                [
                    lambda: slope, lambda: slope * scaled, lambda: slope * after,
                    lambda: slope * (1.0 - bounded * bounded), lambda: slope * before,
                ]
            ):
                wide = make()
                high, less = split(wide)
                rows[assets * g : assets * (g + 1), here] = high
                rows[assets * (5 + g) : assets * (6 + g), here] = less
                flow_acc[assets * g : assets * (g + 1), :] += wide * paid
            slopes[:, here] = slope
        if half == 0:
            return
        basket = sum(part[pl.ds(i, chunks, stride=8), :] for i in range(8))
        x = (basket - 1.0) * (1.0 / soft_width)
        decay = jnp.exp(-jnp.abs(x))
        reward = (notional * soft_width) * (jnp.maximum(x, 0.0) + jnp.log1p(decay))
        inverse = 1.0 / (1.0 + decay)
        sigmoid = jnp.where(x >= 0.0, inverse, decay * inverse)
        pull = notional * flag * sigmoid
        value_all[line, :] = flag * reward
        pull_all[line, :] = pull
        flow_hi = flow.astype(BF16).astype(F32)
        pull_hi = pull.astype(BF16).astype(F32)
        pull_sum = 0.0
        for c in range(chunks):
            here = pl.ds(c * LANES, LANES)
            for index, row in enumerate([flow_hi, flow - flow_hi, rest, pull_hi, pull - pull_hi]):
                target[index : index + 1, here] = row[c : c + 1, :]
            pull_sum = pull_sum + slopes[:, here] * jnp.broadcast_to(pull[c : c + 1, :], (assets, LANES))
        pull_acc[...] += pull_sum
        rows[aim : aim + 16, :] = target[...].astype(BF16)

    cut = 2 * features

    def multiply(rows, part):
        at = slice(0, cut) if part == 0 else slice(cut, low)
        acc[at, :] += lax.dot_general(
            rows[at, :], rows[base:, :], CONTRACT_LAST, preferred_element_type=F32
        )

    def both(index, carry):
        pair(index).wait()
        for part in range(2):
            fill(2 * index, rows_a, part)
            multiply(rows_b, part)
        for part in range(2):
            fill(2 * index + 1, rows_b, part)
            multiply(rows_a, part)
        for copy in leave(index):
            copy.start()
        return carry

    lax.fori_loop(0, blocks // 2, both, 0)
    multiply(rows_b, 0)
    multiply(rows_b, 1)

    mid = features // 2
    high = acc[base:low, 0:features]
    cross = acc[base:low, features:]
    edge = lax.broadcasted_iota(jnp.int32, (features, features), 1) == features - 1
    half = 0.5 * high + jnp.where(edge, 0.0, cross)
    gram = half + half.T
    turned = pltpu.roll(gram[mid:, :], mid, 1)
    lanes = lax.broadcasted_iota(jnp.int32, (mid, features), 1)
    subs = lax.broadcasted_iota(jnp.int32, (mid, features), 0)
    packed = jnp.where(lanes >= subs, gram[0:mid, :], turned)
    keep[0:mid, :] = packed
    give[0:mid, :] = packed
    corner = jnp.sum(jnp.where(lanes == subs, turned, 0.0), axis=0, keepdims=True)
    aimed = acc[aim : aim + 8, 0:features] + jnp.where(edge[0:8], 0.0, acc[aim : aim + 8, features:])
    aims = jnp.concatenate(
        [
            aimed[0:1] + aimed[1:2], aimed[2:3], aimed[3:4] + aimed[4:5],
            jnp.zeros((5, features), F32),
        ],
        axis=0,
    )
    rank = lax.broadcasted_iota(jnp.int32, (8, features), 0)
    packed = jnp.where(rank == 3, jnp.broadcast_to(corner, (8, features)), aims)
    keep[mid : mid + 8, :] = packed
    give[mid : mid + 8, :] = packed
    five = 5 * assets
    edge = edge[0:1]
    leaned = acc[0:five, features:]
    full = acc[0:five, 0:features] + acc[five:aim, 0:features] + jnp.where(edge, 0.0, leaned)
    rest = jnp.sum(jnp.where(edge, leaned + acc[five:aim, features:], 0.0), axis=1, keepdims=True)
    flow = jnp.sum(flow_acc[...], axis=1, keepdims=True)
    pull = jnp.sum(pull_acc[...], axis=1, keepdims=True)
    jac[0:five, :] = full
    slots = lax.broadcasted_iota(jnp.int32, (five, features), 1)
    pull = jnp.concatenate([pull, jnp.zeros((4 * assets, 1), F32)], axis=0)
    sides = jnp.where(
        slots == 0, flow, jnp.where(slots == 1, rest, jnp.where(slots == 2, pull, 0.0))
    ).T
    jac[five : five + 8, :] = sides[0:8, 0:features]
    jac[five + 8 : five + 16, :] = jnp.concatenate(
        [sides[0:8, features:], jnp.zeros((8, features - assets), F32)], axis=1
    )
    mine, other = halves(jac.shape[0] // 2)
    keep[mid + 8 :, :] = jac[mine, :]
    give[mid + 8 :, :] = jac[other, :]
    last_copies = [
        pltpu.make_async_copy(give, give_out, sems.at[0]),
        pltpu.make_async_copy(keep, keep_out, sems.at[1]),
    ]
    for copy in last_copies:
        copy.start()
    for copy in last_copies:
        copy.wait()
    for index in range(blocks // 2):
        for copy in leave(index):
            copy.wait()


def lane(block, index):
    return jnp.broadcast_to(block[:, index : index + 1], block.shape)


def solve_kernel(packed, out, spread):
    features = packed.shape[1]
    blocks = features // 8
    mid = features // 2
    lanes = lax.broadcasted_iota(jnp.int32, (mid, features), 1)
    subs = lax.broadcasted_iota(jnp.int32, (mid, features), 0)
    upper = packed[0:mid, :]
    aims = packed[mid:, :]
    corner = jnp.broadcast_to(aims[3:4], (mid, features))
    lower = jnp.where(lanes < subs, upper, jnp.where(lanes == subs, 0.5 * corner, 0.0))
    half = jnp.concatenate(
        [
            jnp.where(lanes == subs, 0.5 * upper, jnp.where(lanes > subs, upper, 0.0)),
            pltpu.roll(lower, mid, 1),
        ],
        axis=0,
    )
    gram = half + half.T
    lanes = lax.broadcasted_iota(jnp.int32, (8, features), 1)
    subs = lax.broadcasted_iota(jnp.int32, (8, features), 0)
    mat = [gram[8 * v : 8 * v + 8, :] for v in range(blocks)] + [aims]
    for k in range(blocks):
        base = 8 * k
        head = mat[k]
        diag = {}
        for j in range(8):
            col = lane(head, base + j)
            spread[0, j] = col
            for i in range(j + 1):
                diag[i, j] = jnp.broadcast_to(spread[0, j, i : i + 1, :], (8, features))
        inside = (lanes >= base) & (lanes < base + 8)
        spread[1, 0] = jnp.where(inside, jnp.where(lanes == base + subs, -1.0, 0.0), head)
        work = [jnp.broadcast_to(spread[1, 0, i : i + 1, :], (8, features)) for i in range(8)]
        inverse, low = {}, {}
        for p in range(0, 8, 2):
            q = p + 1
            one, off, two = diag[p, p], diag[p, q], diag[q, q]
            inv = 1.0 / (one * two - off * off)
            inverse[p] = (two * inv, off * inv, one * inv)
            lift = {}
            for j in range(q + 1, 8):
                first, second = diag[p, j], diag[q, j]
                lift[j] = (two * first - off * second, one * second - off * first)
                low[p, j], low[q, j] = lift[j][0] * inv, lift[j][1] * inv
            for i in range(q + 1, 8):
                for j in range(i, 8):
                    drop = lift[i][0] * diag[p, j] + lift[i][1] * diag[q, j]
                    diag[i, j] = diag[i, j] - drop * inv
                work[i] = work[i] - (low[p, i] * work[p] + low[q, i] * work[q])
        for p in (6, 4, 2, 0):
            q = p + 1
            one, off, two = inverse[p]
            first = one * work[p] - off * work[q]
            second = two * work[q] - off * work[p]
            for j in reversed(range(q + 1, 8)):
                first = first - low[p, j] * work[j]
                second = second - low[q, j] * work[j]
            work[p], work[q] = first, second
        for v in range(k + 1, blocks + 1):
            new = jnp.where(inside, 0.0, mat[v])
            for c in reversed(range(8)):
                new = new - lane(mat[v], base + c) * work[c]
            mat[v] = new
    kept = jnp.broadcast_to(aims[2:3], (8, features))
    out[...] = jnp.where(subs == 3, kept, mat[blocks])


def adjoint_kernel(
    assets, width,
    solved, jac_mine, jac_other, spot, vol, weights, cash, taken,
    value_in, pull_in, scaled_in, bounded_in,
    value_out, flow_out, greeks_out, cot_out,
    coef, part, line, tangents, cot, jac, values, flows, greeks, sent,
):
    features = 4 * assets
    paths = scaled_in.shape[1]
    chunks = width // LANES
    turned = solved[...].T
    spread = column(vol[...] * root_time, assets)
    base = column(spot[...], assets)
    weight = column(weights[...], assets)
    total = jnp.sum(weights[...] * spot[...], axis=1, keepdims=True)
    offsets = []
    for which in range(2):
        parts = [
            jnp.broadcast_to(turned[assets * g : assets * (g + 1), which : which + 1], (assets, LANES))
            for g in range(4)
        ]
        for g in range(4):
            coef[5 * which + g] = parts[g]
        coef[5 * which + 4] = pltpu.roll(parts[2], 1, 0)
        offsets.append(jnp.sum(parts[1], axis=0, keepdims=True))
    coef[10] = 1.0 / (base * spread)
    coef[11] = weight / jnp.broadcast_to(total, (assets, LANES))

    def leave(index):
        at = pl.ds(pl.multiple_of(index * (2 * width), 2 * width), 2 * width)
        rows = pl.ds(pl.multiple_of(index * (2 * chunks), 2 * chunks), 2 * chunks)
        return [
            pltpu.make_async_copy(cot.at[:, at], cot_out.at[:, at], sent.at[0, index]),
            pltpu.make_async_copy(values.at[rows, :], value_out.at[rows, :], sent.at[1, index]),
            pltpu.make_async_copy(flows.at[rows, :], flow_out.at[rows, :], sent.at[2, index]),
        ]

    def block(index, slot):
        for c in range(chunks):
            at = pl.ds(pl.multiple_of(index * width, width) + c * LANES, LANES)
            here = pl.ds(c * LANES, LANES)
            scaled = scaled_in[:, at]
            bounded = bounded_in[:, at]
            after = pltpu.roll(scaled, assets - 1, 0)
            before = pltpu.roll(scaled, 1, 0)
            curve = 1.0 - bounded * bounded
            for which in range(2):
                k = 5 * which
                bend = coef[k + 1] * scaled
                inner = coef[k] + bend + coef[k + 2] * after
                terms = scaled * inner + coef[k + 3] * bounded
                part[slot, which, 8 * c : 8 * c + 8, :] = sum(
                    terms[8 * g : 8 * g + 8] for g in range(assets // 8)
                )
                tangents[slot, which, :, here] = (
                    inner + bend + coef[k + 4] * before + coef[k + 3] * curve
                )
        at = pl.ds(pl.multiple_of(index * chunks, chunks), chunks)
        fitted = [
            sum(part[slot, which, pl.ds(i, chunks, stride=8), :] for i in range(8)) - offsets[which]
            for which in range(2)
        ]
        rest = 1.0 - taken[at, :].astype(F32)
        values[at, :] = value_in[at, :] + rest * fitted[0]
        flows[at, :] = fitted[1]
        line[slot, 0] = cash[at, :] - fitted[0]
        line[slot, 1] = rest - fitted[1]
        line[slot, 2] = pull_in[at, :]
        for c in range(chunks):
            at = pl.ds(pl.multiple_of(index * width, width) + c * LANES, LANES)
            here = pl.ds(c * LANES, LANES)
            miss, gap, pull = (
                jnp.broadcast_to(line[slot, i, c : c + 1, :], (assets, LANES)) for i in range(3)
            )
            cot[:, at] = (
                miss * tangents[slot, 1, :, here] + gap * tangents[slot, 0, :, here]
            ) * coef[10] + pull * coef[11]

    def both(index, carry):
        block(2 * index, 0)
        block(2 * index + 1, 1)
        for copy in leave(index):
            copy.start()
        return carry

    mine, other = halves(jac_mine.shape[0])
    jac[mine, :] = jac_mine[...]
    jac[other, :] = jac_other[...]
    regression, multiplier = solved[0:1, :], solved[1:2, :]
    aims = features + assets
    against = lax.dot_general(
        solved[...], jac[0:aims, :], CONTRACT_LAST,
        precision=lax.Precision.HIGHEST, preferred_element_type=F32,
    )
    miss = jac[aims : aims + 1, :] - against[0:1, 0:features]
    gap = jac[aims + 1 : aims + 2, :] - against[1:2, 0:features]
    miss_side = jac[aims + 8 : aims + 9, 0:assets] - against[0:1, features:]
    gap_side = jac[aims + 9 : aims + 10, 0:assets] - against[1:2, features:]
    lanes = lax.broadcasted_iota(jnp.int32, (1, LANES), 1)
    double = jnp.where((lanes >= assets) & (lanes < 2 * assets), 2.0, 1.0)
    total = double * (multiplier * miss + regression * gap)
    total = total + pltpu.roll(total, 2 * assets, 1)
    total = total + pltpu.roll(total, assets, 1)

    def earlier(row):
        moved = pltpu.roll(row, features - 2 * assets + 1, 1)
        wrapped = pltpu.roll(row, features - 3 * assets + 1, 1)
        return jnp.where(lanes == 0, wrapped, moved)

    side = earlier(multiplier)[:, 0:assets] * miss_side + earlier(regression)[:, 0:assets] * gap_side
    vega = (total[:, 0:assets] + side) / vol[...]
    pulled_slope = jac[aims + 2 : aims + 3, 0:assets]
    pulled_scaled = solved[3:4, 0:assets]
    pulled = solved[3:4, features - 1 : features]
    value = weights[...] * spot[...]
    whole = jnp.sum(value, axis=1, keepdims=True)
    growth = pulled + vol[...] * root_time * pulled_scaled
    mean = jnp.sum(value * growth, axis=1, keepdims=True) / whole
    delta = weights[...] / whole * (growth - mean)
    vega = vega + value * root_time / whole * (pulled_slope + pulled_scaled)
    greeks[...] = jnp.concatenate([delta, vega], axis=0)
    whole_copy = pltpu.make_async_copy(greeks, greeks_out, sent.at[3, 0])
    whole_copy.start()
    lax.fori_loop(0, paths // (2 * width), both, 0)
    whole_copy.wait()
    for index in range(paths // (2 * width)):
        for copy in leave(index):
            copy.wait()


def swap(value, mask):
    count = math.prod(lax.axis_size(axis) for axis in AXES)
    return lax.ppermute(value, AXES, [(i, i ^ mask) for i in range(count)])


def gather_sum(value, masks):
    combos = [0]
    for mask in masks:
        combos = combos + [c ^ mask for c in combos]
    terms = [value] + [swap(value, c) for c in combos[1:]]
    while len(terms) > 1:
        terms = [a + b for a, b in zip(terms[::2], terms[1::2])]
    return terms[0]


def per_device(normals, spot, vol, weights, cash, taken):
    assets, paths = normals.shape
    features = 4 * assets
    path_total = paths * lax.axis_size("grp") * lax.axis_size("path")
    spot, vol, weights = (a.reshape(1, assets) for a in (spot, vol, weights))
    params = pltpu.CompilerParams(vmem_limit_bytes=16 * 1024 * 1024)
    big = jax.ShapeDtypeStruct((assets, paths), F32)
    jac_rows = features + assets + 16
    gram_rows = features // 2 + 8
    sent = jax.ShapeDtypeStruct((gram_rows + jac_rows // 2, features), F32)
    compact = (paths // LANES, LANES)
    block = 8 * LANES
    remote = pl.BlockSpec(memory_space=pltpu.HBM)
    local = pl.BlockSpec(memory_space=pltpu.VMEM)
    short = jax.ShapeDtypeStruct(compact, F32)
    wide = 16 * LANES
    rows = pltpu.VMEM((10 * assets + 16 + 2 * features, wide), BF16)
    scaled, bounded, value, pull, keep, give = pl.pallas_call(
        functools.partial(sums_kernel, assets, wide),
        in_specs=[remote] * 6,
        out_specs=[remote] * 6,
        out_shape=[
            big, big, short, short,
            sent, sent,
        ],
        scratch_shapes=[
            pltpu.VMEM((8, assets), F32),
            pltpu.VMEM(compact, F32),
            pltpu.VMEM(compact, jnp.int32),
            pltpu.VMEM((assets, paths), F32),
            pltpu.VMEM((4, assets, LANES), F32),
            pltpu.VMEM((wide // 16 + 8, LANES), F32),
            pltpu.VMEM((16, wide), F32),
            pltpu.VMEM((assets, paths), F32),
            pltpu.VMEM((assets, paths), F32),
            pltpu.VMEM(compact, F32),
            pltpu.VMEM(compact, F32),
            pltpu.VMEM(sent.shape, F32),
            pltpu.VMEM(sent.shape, F32),
            pltpu.VMEM((assets, wide), F32),
            rows, rows,
            pltpu.VMEM((10 * assets + 16 + features, 2 * features), F32),
            pltpu.VMEM((5 * assets, LANES), F32),
            pltpu.VMEM((assets, LANES), F32),
            pltpu.VMEM((jac_rows, features), F32),
            pltpu.SemaphoreType.DMA((5 + paths // (2 * wide),)),
            pltpu.SemaphoreType.DMA((4, paths // (2 * wide))),
        ],
        compiler_params=pltpu.CompilerParams(vmem_limit_bytes=60 * 1024 * 1024),
        name="sums",
    )(spot, vol, weights, cash.reshape(compact), taken.reshape(compact), normals)
    sizes = [lax.axis_size(axis) for axis in AXES]
    masks = [1 << bit for bit in range(math.prod(sizes).bit_length() - 1)]
    assert math.prod(sizes) == 1 << len(masks)
    scale = 1.0 / path_total
    packed = lax.optimization_barrier(keep * scale) + swap(give, masks[0]) * scale
    for group in [[masks[1], masks[-1]]] + [[mask] for mask in masks[2:-1]]:
        packed = gather_sum(packed, group)
    gram, jac_mine = packed[:gram_rows], packed[gram_rows:]
    jac_other = swap(jac_mine, masks[0])
    solved = pl.pallas_call(
        solve_kernel,
        out_shape=jax.ShapeDtypeStruct((8, features), F32),
        scratch_shapes=[pltpu.VMEM((2, 8, 8, features), F32)],
        compiler_params=params,
        cost_estimate=pl.CostEstimate(
            flops=4 * 10**9, bytes_accessed=15 * 10**6, transcendentals=features
        ),
        name="solve",
    )(gram)
    value, flow, greeks, cot = pl.pallas_call(
        functools.partial(adjoint_kernel, assets, wide),
        in_specs=[local] * 12,
        out_specs=[remote] * 4,
        out_shape=[short, short, jax.ShapeDtypeStruct((2, assets), F32), big],
        scratch_shapes=[
            pltpu.VMEM((12, assets, LANES), F32),
            pltpu.VMEM((2, 2, wide // 16 + 8, LANES), F32),
            pltpu.VMEM((2, 3, wide // LANES, LANES), F32),
            pltpu.VMEM((2, 2, assets, wide), F32),
            pltpu.VMEM((assets, paths), F32),
            pltpu.VMEM((jac_rows, features), F32),
            pltpu.VMEM(compact, F32),
            pltpu.VMEM(compact, F32),
            pltpu.VMEM((2, assets), F32),
            pltpu.SemaphoreType.DMA((4, paths // (2 * wide))),
        ],
        compiler_params=params,
        name="adjoint",
    )(
        solved, jac_mine, jac_other, spot, vol, weights, cash.reshape(compact), taken.reshape(compact),
        value, pull, scaled, bounded,
    )
    return value.reshape(paths), cot, flow.reshape(paths), greeks


def solution(mesh):
    in_specs = (P(None, ("grp", "path")), P(), P(), P(), P(("grp", "path")), P(("grp", "path")))
    out_specs = (P(("grp", "path")), P(None, ("grp", "path")), P(("grp", "path")), P())
    return jax.shard_map(
        per_device, mesh=mesh, in_specs=in_specs, out_specs=out_specs, check_vma=False
    )
```
